512 devices in a mesh: dp: 16 (over z), pair: 32 (over y, x, core).
Axes of the slice: x: 4, y: 4, z: 16, core: 2. Of those that a mesh axis runs over, the one named last changes fastest.
Arguments:
- embeddings: bfloat16 [16384, 768], P('dp'), may hold values from -4 to 4
- block_sizes: int32 [128], replicated, may hold values from 1 to 128
- fetch_blocks: int32 [16, 32, 16], P('dp', 'pair'), may hold values from 0 to 7
- partners: int32 [16, 32, 16, 4], P('dp', 'pair'), may hold values from 0 to 7, as said below
Outputs:
- weighted_sums: float32 [16384, 768], P(('dp', 'pair'))
- log_mass: float32 [16384], P(('dp', 'pair'))
The draws below stay inside these ranges and needn't reach their ends.
Inputs may be any that keep to these rules, and one draw needn't show every extreme that they name: `partners`: the 4 entries of one worker and owner are different blocks.
All inputs are finite; a program needn't handle non-finite values.
Results may differ from the reference program's by a relative error of at most 0.002.
Values may be sent and summed in bfloat16 or wider, within the bound.
A program may use at most 64 MiB of HBM per device.

```python
import math
import jax
import jax.numpy as jnp
from jax import lax

E = 768
BLK = 128
NB_DEV = 8
PER_SLOT = 4
NBLK = 128
N_DP = 16
N_PAIR = 32


latent_dims = 8


spread = 0.44


def draw_partners(key, part):
    key = jax.random.fold_in(key, 11)
    scores = jax.random.randint(key, (N_DP, N_PAIR, N_DP, NB_DEV), 0, 4096)
    scores = scores * NB_DEV + jnp.arange(NB_DEV, dtype=jnp.int32)
    order = jnp.argsort(scores, axis=-1)
    return order[..., :PER_SLOT].astype(jnp.int32)


def draw_embeddings(key, part):
    key = jax.random.fold_in(key, 5)
    subkeys = jax.random.split(key, 6)
    block_count = N_DP * NB_DEV
    row_count = block_count * BLK
    directions = jax.random.normal(subkeys[0], (latent_dims, E), jnp.float32) / math.sqrt(E)
    centre = jax.random.normal(subkeys[1], (1, 1, E), jnp.float32) / math.sqrt(E)
    offsets = jax.random.normal(subkeys[2], (block_count, 1, E), jnp.float32) * math.sqrt(0.4 / E)
    latent = jax.random.normal(subkeys[3], (row_count, latent_dims), jnp.float32)
    radius = jnp.exp(jax.random.uniform(subkeys[4], (row_count, 1), jnp.float32, math.log(0.75), math.log(1.3)))
    jitter = jax.random.normal(subkeys[5], (row_count, E), jnp.float32) * math.sqrt(0.25 / E)
    spread_rows = latent[:, 0:1] * directions[0][None, :]
    for column in range(1, latent_dims):
        spread_rows = spread_rows + latent[:, column:column + 1] * directions[column][None, :]
    centres = jnp.broadcast_to(centre + offsets, (block_count, BLK, E)).reshape(row_count, E)
    values = centres + spread * radius * spread_rows + jitter
    return jnp.clip(values, -4.0, 4.0).astype(jnp.bfloat16)


def touch_ends(drawn, own_key, least, largest):
    dims = drawn.shape
    index_at = [jax.random.randint(jax.random.fold_in(own_key, axis), (), 0, dims[axis]) for axis in range(len(dims))]
    drawn = drawn.at[tuple(index_at)].set(least)
    longest = dims.index(max(dims))
    index_at[longest] = (index_at[longest] + 1) % dims[longest]
    return drawn.at[tuple(index_at)].set(largest)


def setup_inputs(seed: int = 0) -> dict:
    splits = jax.random.split(jax.random.key(seed), 5)
    embeddings = draw_embeddings(jax.random.fold_in(splits[4], 71), 0)
    block_sizes = touch_ends(jax.random.randint(splits[1], (NBLK,), 1, BLK + 1), jax.random.fold_in(splits[1], 1), 1, BLK).astype(jnp.int32)
    fetch_blocks = touch_ends(jax.random.randint(splits[2], (N_DP, N_PAIR, N_DP), 0, NB_DEV), jax.random.fold_in(splits[2], 1), 0, NB_DEV - 1).astype(jnp.int32)
    partners = draw_partners(jax.random.fold_in(splits[4], 71), 0)
    return dict(embeddings=embeddings, block_sizes=block_sizes, fetch_blocks=fetch_blocks, partners=partners)


inv_band = 1.0


def reference(embeddings, block_sizes, fetch_blocks, partners):
    blocks = embeddings.reshape(N_DP * NB_DEV, BLK, E)
    norms = jnp.sum(jnp.square(blocks.astype(jnp.float32)), axis=2)
    lanes = jnp.arange(BLK, dtype=jnp.int32)
    live = (lanes[None, :] < block_sizes[:, None]).astype(jnp.float32)
    owners = jnp.arange(N_DP, dtype=jnp.int32)
    far = owners[None, None, :] * NB_DEV + fetch_blocks
    near = owners[:, None, None, None] * NB_DEV + partners
    far_flat = far.reshape(-1).astype(jnp.int32)
    near_flat = near.reshape(-1, PER_SLOT).astype(jnp.int32)

    def visit(carry, item):
        sums, mass = carry
        far_id, near_ids = item
        near_rows = blocks[near_ids].astype(jnp.float32)
        far_rows = blocks[far_id].astype(jnp.float32)
        dots = jnp.einsum('pie,je->pij', near_rows, far_rows, precision=lax.Precision.HIGHEST)
        dist = norms[near_ids][:, :, None] + norms[far_id][None, None, :] - 2.0 * dots
        kern = jnp.exp(-inv_band * dist) * live[near_ids][:, :, None] * live[far_id][None, None, :]
        weights = lax.optimization_barrier(kern.astype(jnp.bfloat16)).astype(jnp.float32)
        near_sum = jnp.einsum('pij,je->pie', weights, far_rows, precision=lax.Precision.HIGHEST)
        far_sum = jnp.einsum('pij,pie->je', weights, near_rows, precision=lax.Precision.HIGHEST)
        sums = sums.at[near_ids].add(near_sum)
        sums = sums.at[far_id].add(far_sum)
        mass = mass.at[near_ids].add(jnp.sum(kern, axis=2))
        mass = mass.at[far_id].add(jnp.sum(kern, axis=(0, 1)))
        return (sums, mass), None

    start = (jnp.zeros((N_DP * NB_DEV, BLK, E), jnp.float32), jnp.zeros((N_DP * NB_DEV, BLK), jnp.float32))
    (sums, mass), _ = lax.scan(visit, start, (far_flat, near_flat))
    return sums.reshape(N_DP * NB_DEV * BLK, E), jnp.log(1.0 + mass.reshape(-1))
```

```python
import jax
import jax.numpy as jnp
from jax import lax
from jax.experimental import pallas as pl
from jax.experimental.pallas import tpu as pltpu
from jax.sharding import PartitionSpec as P

MESH = pl.DeviceIdType.MESH
F32, BF16, I32 = jnp.float32, jnp.bfloat16, jnp.int32

OWNERS, COUNT, DEPTH, WIDTH = 16, 8, 128, 768
SIDE = 4
CHIPS = SIDE * SIDE
SHARD = 32
ROWS = CHIPS * SHARD
PAIR = 2 * SHARD
GROUP = 4
COLS = GROUP * PAIR
WIDE = WIDTH + 128
FAR = 1e30

KIDS = {0: (2, 1), 2: (5, 3), 5: (8, 7, 4, 6)}
SLOTS = (0, 2, -2, 1, -1, 5, -5, 3, -3, 8, 7, -7, 4, -4, 6, -6)
SLOT = {d: s for s, d in enumerate(SLOTS)}
SLOT[-8] = SLOT[8]
REACH = 3
EDGES = {}
for parent, kids in KIDS.items():
    for kid in kids:
        for sign in (1, -1):
            EDGES[sign * kid] = sign * parent
EDGE = {d: e for e, d in enumerate(EDGES)}


def below(parent):
    sign = -1 if parent < 0 else 1
    kids = KIDS.get(abs(parent), ())
    if parent == 0:
        return [s * k for k in kids for s in (1, -1)]
    return [sign * k for k in kids]


OFFSETS = [(dx, dy) for dy in (2, 1, 3, 0) for dx in (2, 1, 3, 0)]
PEERS = [o for o in OFFSETS if o != (0, 0)]


def kernel(emb, bs_hbm, fetch_hbm, part_hbm, out_ref, log_ref, xz, cols, kern, acc, mass, ni, sizes, fetch, part,
           mown, mpair, mplane, cm, sg, send, recv, loc_sem, e_send, e_recv, d_send, d_recv, c_send, c_recv,
           m_send, m_recv, r_send, r_recv):
    z = lax.axis_index("dp")
    p = lax.axis_index("pair")
    core = lax.rem(p, 2)
    chip = p // 2
    x = lax.rem(chip, SIDE)
    y = chip // SIDE
    half = chip // 2

    def along(d):
        return (lax.rem(z + d + OWNERS, OWNERS), p)

    def place(dx, dy):
        return lax.rem(y + dy, SIDE) * SIDE + lax.rem(x + dx, SIDE)

    def peer(dx, dy):
        return (z, place(dx, dy) * 2 + core)

    other = (z, chip * 2 + 1 - core)

    barrier = pltpu.get_barrier_semaphore()
    for d in range(1, REACH + 1):
        for s in (1, -1):
            pl.semaphore_signal(barrier, 1, device_id=along(s * d), device_id_type=MESH)
    for dx, dy in PEERS:
        pl.semaphore_signal(barrier, 1, device_id=peer(dx, dy), device_id_type=MESH)
    pl.semaphore_signal(barrier, 1, device_id=other, device_id_type=MESH)

    loads = [
        pltpu.make_async_copy(fetch_hbm, fetch, loc_sem.at[0]),
        pltpu.make_async_copy(part_hbm, part, loc_sem.at[1]),
        pltpu.make_async_copy(bs_hbm, sizes, loc_sem.at[2]),
        pltpu.make_async_copy(emb.at[:, core], xz, loc_sem.at[3]),
        pltpu.make_async_copy(emb.at[chip, core], cols.at[0, 0], loc_sem.at[4]),
        pltpu.make_async_copy(emb.at[chip, 1 - core], cols.at[0, 1], loc_sem.at[5]),
    ]
    for c in loads:
        c.start()
    pl.semaphore_wait(barrier, 2 * REACH + len(PEERS) + 1)

    sent = []

    def go(c):
        c.start()
        sent.append(c)

    def span(d):
        return (0, 16) if d == 8 else (16, 16) if d == -8 else (0, SHARD)

    def rows_copy(d):
        parent = EDGES[d]
        r0, nr = span(d)
        src = emb.at[chip, core, pl.ds(r0, nr)] if parent == 0 else cols.at[SLOT[parent], 0, pl.ds(r0, nr)]
        return pltpu.make_async_remote_copy(
            src_ref=src, dst_ref=cols.at[SLOT[d], 0, pl.ds(r0, nr)], send_sem=e_send.at[EDGE[d]],
            recv_sem=e_recv.at[EDGE[d]], device_id=along(d - parent), device_id_type=MESH)

    def twin_copy(s):
        return pltpu.make_async_remote_copy(
            src_ref=cols.at[s, 0], dst_ref=cols.at[s, 1], send_sem=d_send.at[s], recv_sem=d_recv.at[s],
            device_id=other, device_id_type=MESH)

    def count_copy(d):
        parent = EDGES[d]
        return pltpu.make_async_remote_copy(
            src_ref=cm.at[SLOT[parent]], dst_ref=cm.at[SLOT[d]], send_sem=c_send.at[EDGE[d]],
            recv_sem=c_recv.at[EDGE[d]], device_id=along(d - parent), device_id_type=MESH)

    def rows_in(*ds):
        for d in ds:
            rows_copy(d).wait_recv()
            for k in below(d):
                go(rows_copy(k))
        for d in ds:
            if d != 8:
                go(twin_copy(SLOT[d]))

    def counts_in(*ds):
        for d in ds:
            count_copy(d).wait_recv()
            for k in below(d):
                if k != -8:
                    go(count_copy(k))

    for d in below(0):
        go(rows_copy(d))

    sub8 = lax.broadcasted_iota(I32, (COUNT, 128), 0)
    lane8 = lax.broadcasted_iota(I32, (COUNT, 128), 1)
    loads[0].wait()
    loads[1].wait()
    hits = jnp.zeros((COUNT, 128), F32)
    for o in range(OWNERS):
        near = sub8 == part[0, 0, o, 0]
        for k in range(1, 4):
            near = jnp.logical_or(near, sub8 == part[0, 0, o, k])
        far = lane8 == o * COUNT + fetch[0, 0, o]
        hits = hits + jnp.where(jnp.logical_and(near, far), 1.0, 0.0)
    mown[...] = hits
    swap = pltpu.make_async_remote_copy(
        src_ref=mown, dst_ref=mpair, send_sem=m_send.at[15], recv_sem=m_recv.at[15], device_id=other,
        device_id_type=MESH)
    go(swap)
    swap.wait_recv()
    mplane[15] = mown[...] + mpair[...]
    plane = []
    for i, (dx, dy) in enumerate(PEERS):
        c = pltpu.make_async_remote_copy(
            src_ref=mplane.at[15], dst_ref=mplane.at[i], send_sem=m_send.at[i], recv_sem=m_recv.at[i],
            device_id=peer(dx, dy), device_id_type=MESH)
        go(c)
        plane.append(c)

    for c in loads[2:]:
        c.wait()
    bs = sizes[...].astype(F32)

    def row_norms(k, carry):
        v = xz[pl.ds(k * 4, 4)].reshape(4 * SHARD, WIDTH).astype(F32)
        n = jnp.sum(v * v, axis=1, keepdims=True)
        t = k * 4 * SHARD + lax.broadcasted_iota(I32, (4 * SHARD, 128), 0)
        lane = lax.broadcasted_iota(I32, (4 * SHARD, 128), 1)
        block = z * COUNT + t // PAIR
        size = jnp.sum(jnp.where(lane == block, bs, 0.0), axis=1, keepdims=True)
        inside = lax.rem(t // SHARD, 2) * PAIR + core * SHARD + lax.rem(t, SHARD)
        dead = inside.astype(F32) >= size
        ni[pl.ds(k * 4 * SHARD, 4 * SHARD)] = n + jnp.where(dead, FAR, 0.0)
        return carry

    lax.fori_loop(0, CHIPS // 4, row_norms, 0)

    lane1 = lax.broadcasted_iota(I32, (1, 128), 1)
    sub128 = lax.broadcasted_iota(I32, (128, 128), 0)
    lane128 = lax.broadcasted_iota(I32, (128, 128), 1)
    row64 = lax.broadcasted_iota(I32, (PAIR, 128), 0)
    mine = row64 < SHARD
    inside64 = lax.rem(chip, 2) * PAIR + jnp.where(mine, core * SHARD + row64, (1 - core) * SHARD + row64 - SHARD)
    inside64 = inside64.astype(F32)

    def block_of(d):
        return lax.rem(z - d + 2 * OWNERS, OWNERS) * COUNT + half

    def far_norms(g):
        parts = []
        for h in range(GROUP // 2):
            two = []
            for s in (g * GROUP + 2 * h, g * GROUP + 2 * h + 1):
                v = cols[s].reshape(PAIR, WIDTH).astype(F32)
                n = jnp.sum(v * v, axis=1, keepdims=True)
                size = jnp.sum(jnp.where(lane1 == block_of(SLOTS[s]), bs, 0.0), axis=1, keepdims=True)
                two.append(n + jnp.where(inside64 >= size, FAR, 0.0))
            n = jnp.concatenate(two, axis=0)
            parts.append(jnp.sum(jnp.where(sub128 == lane128, n, 0.0), axis=0, keepdims=True))
        return jnp.concatenate(parts, axis=1)

    def near(g):
        for s in range(g * GROUP, (g + 1) * GROUP):
            if s:
                twin_copy(s).wait_recv()
        far = cols[pl.ds(g * GROUP, GROUP)].reshape(COLS, WIDTH)
        nj = far_norms(g)

        def part_of(k, carry):
            r = pl.ds(k * 128, 128)
            v = xz[pl.ds(k * 4, 4)].reshape(128, WIDTH)
            dots = lax.dot_general(v, far, (((1,), (1,)), ((), ())), preferred_element_type=F32)
            n = ni[r]
            dist = jnp.concatenate([n, n], axis=1) + nj - 2.0 * dots
            kern[g, r] = jnp.exp(-dist)
            return carry

        lax.fori_loop(0, ROWS // 128, part_of, 0)

    def counts(g):
        out = []
        for h in range(GROUP // 2):
            two = []
            for s in (g * GROUP + 2 * h, g * GROUP + 2 * h + 1):
                there = cm[s, pl.ds(half, 1), :]
                here = jnp.where(lane8 == block_of(SLOTS[s]), cm[0], 0.0)
                both = here + jnp.where(lane8 == z * COUNT + sub8, there, 0.0)
                two.append(jnp.sum(both, axis=1, keepdims=True))
            out.append(jnp.where(lane8 < PAIR, two[0], two[1]))
        sg[g] = jnp.concatenate(out, axis=1)

    def part_sums(g, r0):
        r = pl.ds(r0, 128)
        k = kern[g, r]
        b0 = r0 // PAIR
        s0 = jnp.broadcast_to(sg[g, pl.ds(b0, 1), :], (PAIR, COLS))
        s1 = jnp.broadcast_to(sg[g, pl.ds(b0 + 1, 1), :], (PAIR, COLS))
        s = jnp.concatenate([s0, s1], axis=0)
        w = s * k.astype(BF16).astype(F32)
        hi = w.astype(BF16)
        lo = (w - hi.astype(F32)).astype(BF16)
        far = cols[pl.ds(g * GROUP, GROUP)].reshape(COLS, WIDTH)
        t = jnp.dot(hi, far, preferred_element_type=F32) + jnp.dot(lo, far, preferred_element_type=F32)
        m = s * k
        m = m[:, :128] + m[:, 128:]
        if g:
            t = t + acc[r]
            m = m + mass[r]
        return t, m

    def sums(g):
        def step(k, carry):
            t, m = part_sums(g, k * 128)
            acc[pl.ds(k * 128, 128)] = t
            mass[pl.ds(k * 128, 128)] = m
            return carry

        lax.fori_loop(0, ROWS // 128, step, 0)

    rows_in(2, -2)
    rows_in(1, -1)
    total = mplane[15]
    for i, c in enumerate(plane):
        c.wait_recv()
        total = total + mplane[i]
    cm[0] = total
    for d in below(0):
        go(count_copy(d))
    near(0)
    rows_in(5, -5)
    rows_in(3, -3)
    counts_in(2, -2, 1, -1)
    counts(0)
    sums(0)
    near(1)
    rows_in(8, -8)
    rows_in(7, -7)
    counts_in(5, -5, 3, -3)
    counts(1)
    sums(1)
    near(2)
    rows_in(4, -4)
    rows_in(6, -6)
    near(3)
    counts_in(8, 7, -7, 4, -4, 6, -6)
    counts(2)
    sums(2)
    counts(3)

    lane32 = lax.broadcasted_iota(I32, (SHARD, 128), 1)
    order = []
    i = 0
    for dy in (2, 1, 3, 0):
        row = lax.rem(y + dy, SIDE)
        t, m = part_sums(3, row * 128)
        acc[pl.ds(row * 128, 128)] = t
        mass[pl.ds(row * 128, 128)] = m
        for dx in (2, 1, 3, 0):
            if (dx, dy) == (0, 0):
                continue
            q = place(dx, dy) * SHARD
            v = acc[pl.ds(q, SHARD)]
            a = jnp.sum(mass[pl.ds(q, SHARD)], axis=1, keepdims=True)
            a0 = a.astype(BF16)
            rest = a - a0.astype(F32)
            a1 = rest.astype(BF16)
            a2 = (rest - a1.astype(F32)).astype(BF16)
            send[i, :, :WIDTH] = v.astype(BF16)
            tail = jnp.where(lane32 == 0, a0.astype(F32),
                             jnp.where(lane32 == 1, a1.astype(F32), jnp.where(lane32 == 2, a2.astype(F32), 0.0)))
            send[i, :, WIDTH:] = tail.astype(BF16)
            c = pltpu.make_async_remote_copy(
                src_ref=send.at[i], dst_ref=recv.at[i], send_sem=r_send.at[i], recv_sem=r_recv.at[i],
                device_id=peer(dx, dy), device_id_type=MESH)
            go(c)
            order.append(c)
            i += 1

    q = chip * SHARD
    v = acc[pl.ds(q, SHARD)]
    a = mass[pl.ds(q, SHARD)]
    for i, c in enumerate(order):
        c.wait_recv()
        v = v + recv[i, :, :WIDTH].astype(F32)
        a = a + recv[i, :, WIDTH:].astype(F32)
    out_ref[...] = v
    m = jnp.log(1.0 + jnp.sum(a, axis=1, keepdims=True))
    sub32 = lax.broadcasted_iota(I32, (SHARD, 128), 0)
    log_ref[...] = jnp.sum(jnp.where(sub32 == lane32, m, 0.0), axis=0, keepdims=True)
    for c in sent:
        c.wait_send()


def body(embeddings, block_sizes, fetch_blocks, partners):
    hbm = pl.BlockSpec(memory_space=pl.ANY)
    vmem = pl.BlockSpec(memory_space=pltpu.VMEM)
    dma = pltpu.SemaphoreType.DMA
    edges = len(EDGES)
    out, logs = pl.pallas_call(
        kernel,
        out_shape=(jax.ShapeDtypeStruct((SHARD, WIDTH), F32), jax.ShapeDtypeStruct((1, 128), F32)),
        in_specs=[hbm] * 4,
        out_specs=(vmem, vmem),
        scratch_shapes=[
            pltpu.VMEM((CHIPS, SHARD, WIDTH), BF16),
            pltpu.VMEM((OWNERS, 2, SHARD, WIDTH), BF16),
            pltpu.VMEM((OWNERS // GROUP, ROWS, COLS), F32),
            pltpu.VMEM((ROWS, WIDTH), F32),
            pltpu.VMEM((ROWS, 128), F32),
            pltpu.VMEM((ROWS, 128), F32),
            pltpu.VMEM((1, 128), I32),
            pltpu.SMEM((1, 1, 16), I32),
            pltpu.SMEM((1, 1, 16, 4), I32),
            pltpu.VMEM((COUNT, 128), F32),
            pltpu.VMEM((COUNT, 128), F32),
            pltpu.VMEM((CHIPS, COUNT, 128), F32),
            pltpu.VMEM((OWNERS, COUNT, 128), F32),
            pltpu.VMEM((OWNERS // GROUP, COUNT, COLS), F32),
            pltpu.VMEM((len(PEERS), SHARD, WIDE), BF16),
            pltpu.VMEM((len(PEERS), SHARD, WIDE), BF16),
            dma((6,)),
            dma((edges,)), dma((edges,)),
            dma((OWNERS,)), dma((OWNERS,)),
            dma((edges,)), dma((edges,)),
            dma((CHIPS,)), dma((CHIPS,)),
            dma((CHIPS,)), dma((CHIPS,)),
        ],
        compiler_params=pltpu.CompilerParams(collective_id=0, has_side_effects=True, vmem_limit_bytes=40 << 20),
        cost_estimate=pl.CostEstimate(flops=3 * 2 * 512 * 1024 * 768, bytes_accessed=4 << 20, transcendentals=512 * 1024),
    )(embeddings.reshape(CHIPS, 2, SHARD, WIDTH), block_sizes.reshape(1, -1), fetch_blocks, partners)
    return out, logs[0, :SHARD]


def solution(mesh):
    return jax.shard_map(
        body,
        mesh=mesh,
        in_specs=(P("dp", None), P(), P("dp", "pair", None), P("dp", "pair", None, None)),
        out_specs=(P(("dp", "pair"), None), P(("dp", "pair"))),
        check_vma=False,
    )
```

```python
import jax
import jax.numpy as jnp
from jax import lax
from jax.experimental import pallas as pl
from jax.experimental.pallas import tpu as pltpu
from jax.sharding import PartitionSpec as P

MESH = pl.DeviceIdType.MESH
F32, BF16, I32 = jnp.float32, jnp.bfloat16, jnp.int32

OWNERS, COUNT, DEPTH, WIDTH = 16, 8, 128, 768
SIDE = 4
CHIPS = SIDE * SIDE
SHARD = 32
ROWS = CHIPS * SHARD
PAIR = 2 * SHARD
GROUP = 4
COLS = GROUP * PAIR
FAR = 1e30

KIDS = {0: (2, 1), 2: (5, 3), 5: (8, 7, 4, 6)}
SLOTS = (0, 2, -2, 1, -1, 5, -5, 3, -3, 8, 7, -7, 4, -4, 6, -6)
SLOT = {d: s for s, d in enumerate(SLOTS)}
SLOT[-8] = SLOT[8]
REACH = 3
COUNT_SEM = {2: 0, -2: 1, 5: 2, -5: 3}
EDGES = {}
for parent, kids in KIDS.items():
    for kid in kids:
        for sign in (1, -1):
            EDGES[sign * kid] = sign * parent
EDGE = {d: e for e, d in enumerate(EDGES)}


def below(parent):
    sign = -1 if parent < 0 else 1
    kids = KIDS.get(abs(parent), ())
    if parent == 0:
        return [s * k for k in kids for s in (1, -1)]
    return [sign * k for k in kids]


ORDER = (2, 1, 3, 0)
OFFSETS = [(dx, dy) for dy in ORDER for dx in ORDER]
PEERS = [o for o in OFFSETS if o != (0, 0)]
MATES = [(dx, dy, dc) for dx, dy in OFFSETS for dc in (0, 1) if (dx, dy, dc) != (0, 0, 0)]


def kernel(emb, ints, out_ref, log_ref, xz, cols, kern, acc, mass, ni, cm, tsum, sg, send, recv, loc_sem, sent,
           e_recv, d_recv, c_recv, m_sem, r_recv, a_recv):
    z = lax.axis_index("dp")
    p = lax.axis_index("pair")
    core = lax.rem(p, 2)
    chip = p // 2
    x = lax.rem(chip, SIDE)
    y = chip // SIDE
    half = chip // 2

    def along(d):
        return (lax.rem(z + d + OWNERS, OWNERS), p)

    def place(dx, dy):
        return lax.rem(y + dy, SIDE) * SIDE + lax.rem(x + dx, SIDE)

    def peer(dx, dy):
        return (z, place(dx, dy) * 2 + core)

    other = (z, chip * 2 + 1 - core)

    barrier = pltpu.get_barrier_semaphore()
    for d in range(1, REACH + 1):
        for s in (1, -1):
            pl.semaphore_signal(barrier, 1, device_id=along(s * d), device_id_type=MESH)
    for dx, dy, dc in MATES:
        mate = (z, place(dx, dy) * 2 + lax.rem(core + dc, 2))
        pl.semaphore_signal(barrier, 1, device_id=mate, device_id_type=MESH)

    loads = [
        pltpu.make_async_copy(emb.at[chip, core], cols.at[pl.ds(0, SHARD)], loc_sem.at[0]),
        pltpu.make_async_copy(emb.at[chip, 1 - core], cols.at[pl.ds(SHARD, SHARD)], loc_sem.at[0]),
    ]
    for k in range(CHIPS):
        loads.append(pltpu.make_async_copy(emb.at[k, core], xz.at[pl.ds(k * SHARD, SHARD)], loc_sem.at[1]))
    for c in loads:
        c.start()

    sub8 = lax.broadcasted_iota(I32, (COUNT, 128), 0)
    lane8 = lax.broadcasted_iota(I32, (COUNT, 128), 1)
    sub128 = lax.broadcasted_iota(I32, (128, 128), 0)
    lane128 = lax.broadcasted_iota(I32, (128, 128), 1)
    spread = jnp.where(lane128 // COUNT == sub128, 1.0, 0.0).astype(BF16)
    wide = jnp.dot(ints[...].astype(BF16), spread, preferred_element_type=F32).astype(I32)
    near = sub8 == wide[2:3]
    for k in range(3, 6):
        near = jnp.logical_or(near, sub8 == wide[k:k + 1])
    far = wide[1:2] == lax.rem(lane8, COUNT)
    cm[0] = jnp.where(jnp.logical_and(near, far), 1.0, 0.0)
    pl.semaphore_wait(barrier, 2 * REACH + len(MATES))

    def span(d):
        return (0, 16) if d == 8 else (16, 16) if d == -8 else (0, SHARD)

    def rows_copy(d):
        parent = EDGES[d]
        r0, nr = span(d)
        if parent == 0:
            src = emb.at[chip, core, pl.ds(r0, nr)]
        else:
            src = cols.at[pl.ds(SLOT[parent] * PAIR + r0, nr)]
        return pltpu.make_async_remote_copy(
            src_ref=src, dst_ref=cols.at[pl.ds(SLOT[d] * PAIR + r0, nr)], send_sem=sent.at[0],
            recv_sem=e_recv.at[EDGE[d]], device_id=along(d - parent), device_id_type=MESH)

    def twin_copy(s):
        return pltpu.make_async_remote_copy(
            src_ref=cols.at[pl.ds(s * PAIR, SHARD)], dst_ref=cols.at[pl.ds(s * PAIR + SHARD, SHARD)],
            send_sem=sent.at[1], recv_sem=d_recv.at[s // GROUP], device_id=other, device_id_type=MESH)

    def count_copy(d):
        parent = EDGES[d]
        return pltpu.make_async_remote_copy(
            src_ref=cm.at[SLOT[parent]], dst_ref=cm.at[SLOT[d]], send_sem=sent.at[2],
            recv_sem=c_recv.at[COUNT_SEM.get(d, 4)], device_id=along(d - parent), device_id_type=MESH)

    def rows_in(*ds):
        for d in ds:
            rows_copy(d).wait_recv()
            for k in below(d):
                rows_copy(k).start()
        for d in ds:
            if d != 8:
                twin_copy(SLOT[d]).start()

    def counts_in(*ds):
        for d in ds:
            count_copy(d).wait_recv()
            for k in below(d):
                if k != -8:
                    count_copy(k).start()

    def rest_in():
        come = cm.at[pl.ds(0, OWNERS - 1 - len(COUNT_SEM))]
        pltpu.make_async_copy(come, come, c_recv.at[4]).wait()

    for d in below(0):
        count_copy(d).start()
    for d in below(0):
        rows_copy(d).start()

    pltpu.make_async_copy(xz, xz, loc_sem.at[1]).wait()
    bs = ints[0:1]
    for k in range(ROWS // 128):
        v = xz[k * 128:(k + 1) * 128].astype(F32)
        n = jnp.sum(v * v, axis=1, keepdims=True)
        t = k * 128 + lax.broadcasted_iota(I32, (128, 128), 0)
        lane = lax.broadcasted_iota(I32, (128, 128), 1)
        size = jnp.sum(jnp.where(lane == z * COUNT + t // PAIR, bs, 0.0), axis=1, keepdims=True)
        inside = lax.rem(t // SHARD, 2) * PAIR + core * SHARD + lax.rem(t, SHARD)
        ni[k * 128:(k + 1) * 128] = n + jnp.where(inside.astype(F32) >= size, FAR, 0.0)

    lane1 = lax.broadcasted_iota(I32, (1, 128), 1)
    row64 = lax.broadcasted_iota(I32, (PAIR, 128), 0)
    mine = row64 < SHARD
    inside64 = lax.rem(chip, 2) * PAIR + jnp.where(mine, core * SHARD + row64, (1 - core) * SHARD + row64 - SHARD)
    inside64 = inside64.astype(F32)

    def owner(d):
        return lax.rem(z - d + 2 * OWNERS, OWNERS)

    def far_norms(g):
        parts = []
        for h in range(GROUP // 2):
            two = []
            for s in (g * GROUP + 2 * h, g * GROUP + 2 * h + 1):
                v = cols[s * PAIR:(s + 1) * PAIR].astype(F32)
                n = jnp.sum(v * v, axis=1, keepdims=True)
                block = owner(SLOTS[s]) * COUNT + half
                size = jnp.sum(jnp.where(lane1 == block, bs, 0.0), axis=1, keepdims=True)
                two.append(n + jnp.where(inside64 >= size, FAR, 0.0))
            n = jnp.concatenate(two, axis=0)
            parts.append(jnp.sum(jnp.where(sub128 == lane128, n, 0.0), axis=0, keepdims=True))
        return jnp.concatenate(parts, axis=1)

    def near(g):
        if g == 0:
            both = cols.at[pl.ds(0, PAIR)]
            pltpu.make_async_copy(both, both, loc_sem.at[0]).wait()
        come = cols.at[pl.ds(0, (GROUP - (g == 0)) * SHARD)]
        pltpu.make_async_copy(come, come, d_recv.at[g]).wait()
        nj = far_norms(g)
        for r in range(0, ROWS, 256):
            dots = lax.dot_general(xz[r:r + 256], cols[g * COLS:(g + 1) * COLS], (((1,), (1,)), ((), ())),
                                   preferred_element_type=F32)
            n = ni[r:r + 256]
            dist = jnp.concatenate([n, n], axis=1) + nj - 2.0 * dots
            kern[r:r + 256, g * COLS:(g + 1) * COLS] = jnp.exp(-dist)

    counts_in(2, -2)
    rows_in(2, -2)
    rows_in(1, -1)
    counts_in(5, -5)
    rows_in(5, -5)
    rows_in(3, -3)
    rest_in()

    slot1 = lane1 // COUNT
    own1 = jnp.zeros((1, 128), I32)
    for s, d in enumerate(SLOTS):
        own1 = jnp.where(slot1 == s, owner(d), own1)
    own1 = own1 * COUNT + lax.rem(lane1, COUNT)
    perm = jnp.where(sub128 == own1, 1.0, 0.0).astype(BF16)
    pick = jnp.where(lane8 == z * COUNT + sub8, 1.0, 0.0).astype(BF16)
    there = cm[...].reshape(OWNERS * COUNT, 128).astype(BF16)
    pairs = jnp.dot(cm[0].astype(BF16), perm, preferred_element_type=F32) + lax.dot_general(
        pick, there, (((1,), (1,)), ((), ())), preferred_element_type=F32)
    tsum[2 * CHIPS - 1] = pairs
    for i, (dx, dy, dc) in enumerate(MATES):
        pltpu.make_async_remote_copy(
            src_ref=tsum.at[2 * CHIPS - 1], dst_ref=tsum.at[i], send_sem=m_sem.at[0], recv_sem=m_sem.at[1],
            device_id=(z, place(dx, dy) * 2 + lax.rem(core + dc, 2)), device_id_type=MESH).start()
    near(0)
    near(1)
    rows_in(8, -8)
    rows_in(7, -7)
    rows_in(4, -4)
    rows_in(6, -6)
    near(2)
    near(3)
    mates = tsum.at[pl.ds(0, len(MATES))]
    pltpu.make_async_copy(mates, mates, m_sem.at[1]).wait()
    total = tsum[2 * CHIPS - 1]
    for i in range(len(MATES)):
        total = total + tsum[i]
    for s in range(0, OWNERS, 2):
        two = [jnp.sum(jnp.where(lane8 == t * COUNT + half, total, 0.0), axis=1, keepdims=True) for t in (s, s + 1)]
        sg[:, s * PAIR:(s + 2) * PAIR] = jnp.where(lane8 < PAIR, two[0], two[1])

    def sums(row, c0, c1):
        k = kern[pl.ds(row * 128, 128), c0:c1]
        s0 = jnp.broadcast_to(sg[pl.ds(row * 2, 1), c0:c1], (PAIR, c1 - c0))
        s1 = jnp.broadcast_to(sg[pl.ds(row * 2 + 1, 1), c0:c1], (PAIR, c1 - c0))
        s = jnp.concatenate([s0, s1], axis=0)
        w = s * k.astype(BF16).astype(F32)
        hi = w.astype(BF16)
        lo = (w - hi.astype(F32)).astype(BF16)
        far = cols[c0:c1]
        t = jnp.dot(hi, far, preferred_element_type=F32) + jnp.dot(lo, far, preferred_element_type=F32)
        m = s * k
        return t, sum(m[:, 128 * h:128 * (h + 1)] for h in range((c1 - c0) // 128))

    lane32 = lax.broadcasted_iota(I32, (SHARD, 128), 1)
    sub32 = lax.broadcasted_iota(I32, (SHARD, 128), 0)
    i = 0
    for dy in ORDER:
        row = lax.rem(y + dy, SIDE)
        r = pl.ds(row * 128, 128)
        t, m = sums(row, 0, 4 * COLS)
        m = jnp.sum(m, axis=1, keepdims=True)
        mass[dy] = jnp.sum(jnp.where(sub128 == lane128, m, 0.0), axis=0, keepdims=True)
        acc[r] = t
        for dx in ORDER:
            if (dx, dy) == (0, 0):
                continue
            send[i] = acc[pl.ds(place(dx, dy) * SHARD, SHARD)].astype(BF16)
            pltpu.make_async_remote_copy(
                src_ref=send.at[i], dst_ref=recv.at[i], send_sem=sent.at[3], recv_sem=r_recv.at[ORDER.index(dy)],
                device_id=peer(dx, dy), device_id_type=MESH).start()
            pltpu.make_async_remote_copy(
                src_ref=mass.at[dy], dst_ref=mass.at[SIDE + i], send_sem=sent.at[4], recv_sem=a_recv.at[0],
                device_id=peer(dx, dy), device_id_type=MESH).start()
            i += 1

    v = acc[pl.ds(chip * SHARD, SHARD)]
    a = mass[0]
    for h in range(SIDE):
        come = pl.ds(h * SIDE, SIDE - (h == SIDE - 1))
        pltpu.make_async_copy(recv.at[come], recv.at[come], r_recv.at[h]).wait()
        for i in range(h * SIDE, min((h + 1) * SIDE, len(PEERS))):
            v = v + recv[i].astype(F32)
    come = mass.at[pl.ds(SIDE, len(PEERS))]
    pltpu.make_async_copy(come, come, a_recv.at[0]).wait()
    for i in range(len(PEERS)):
        a = a + mass[SIDE + i]
    out_ref[...] = v
    m = jnp.sum(jnp.where(lane32 == x * SHARD + sub32, a, 0.0), axis=1, keepdims=True)
    m = jnp.log(1.0 + m)
    log_ref[...] = jnp.sum(jnp.where(sub32 == lane32, m, 0.0), axis=0, keepdims=True)
    shards = cols.at[pl.ds(0, (OWNERS - 1) * SHARD)]
    counted = cm.at[pl.ds(0, OWNERS - 1)]
    for what, sem in ((shards, sent.at[0]), (shards, sent.at[1]), (counted, sent.at[2]), (send, sent.at[3]),
                      (come, sent.at[4]), (mates, m_sem.at[0])):
        pltpu.make_async_copy(what, what, sem).wait()


def body(embeddings, block_sizes, fetch_blocks, partners):
    hbm = pl.BlockSpec(memory_space=pltpu.HBM)
    vmem = pl.BlockSpec(memory_space=pltpu.VMEM)
    dma = pltpu.SemaphoreType.DMA
    edges = len(EDGES)
    room = ((0, 0), (0, 128 - OWNERS))
    ints = jnp.concatenate([
        block_sizes.reshape(1, 128),
        jnp.pad(fetch_blocks.reshape(1, OWNERS), room),
        jnp.pad(jnp.swapaxes(partners, 2, 3).reshape(4, OWNERS), room),
        jnp.zeros((2, 128), I32),
    ]).astype(F32)
    out, logs = pl.pallas_call(
        kernel,
        out_shape=(jax.ShapeDtypeStruct((SHARD, WIDTH), F32), jax.ShapeDtypeStruct((1, 128), F32)),
        in_specs=[hbm, vmem],
        out_specs=(vmem, vmem),
        scratch_shapes=[
            pltpu.VMEM((ROWS, WIDTH), BF16),
            pltpu.VMEM((OWNERS * PAIR, WIDTH), BF16),
            pltpu.VMEM((ROWS, OWNERS * PAIR), F32),
            pltpu.VMEM((ROWS, WIDTH), F32),
            pltpu.VMEM((SIDE + len(PEERS), 1, 128), F32),
            pltpu.VMEM((ROWS, 128), F32),
            pltpu.VMEM((OWNERS, COUNT, 128), F32),
            pltpu.VMEM((2 * CHIPS, COUNT, 128), F32),
            pltpu.VMEM((COUNT, OWNERS * PAIR), F32),
            pltpu.VMEM((len(PEERS), SHARD, WIDTH), BF16),
            pltpu.VMEM((len(PEERS), SHARD, WIDTH), BF16),
            dma((2,)),
            dma((5,)),
            dma((edges,)),
            dma((OWNERS // GROUP,)),
            dma((len(COUNT_SEM) + 1,)),
            dma((2,)),
            dma((SIDE,)),
            dma((1,)),
        ],
        compiler_params=pltpu.CompilerParams(collective_id=0, has_side_effects=True, vmem_limit_bytes=53 << 20),
        cost_estimate=pl.CostEstimate(flops=3 * 2 * 512 * 1024 * 768, bytes_accessed=4 << 20, transcendentals=512 * 1024),
    )(embeddings.reshape(CHIPS, 2, SHARD, WIDTH), ints)
    return out, logs[0, :SHARD]


def solution(mesh):
    return jax.shard_map(
        body,
        mesh=mesh,
        in_specs=(P("dp", None), P(), P("dp", "pair", None), P("dp", "pair", None, None)),
        out_specs=(P(("dp", "pair"), None), P(("dp", "pair"))),
        check_vma=False,
    )
```

```python
import jax
import jax.numpy as jnp
from jax import lax
from jax.experimental import pallas as pl
from jax.experimental.pallas import tpu as pltpu
from jax.sharding import PartitionSpec as P

MESH = pl.DeviceIdType.MESH
F32, BF16, I32 = jnp.float32, jnp.bfloat16, jnp.int32

OWNERS, COUNT, DEPTH, WIDTH = 16, 8, 128, 768
SIDE = 4
CHIPS = SIDE * SIDE
SHARD = 32
ROWS = CHIPS * SHARD
PAIR = 2 * SHARD
GROUP = 4
CUT = 512
COLS = GROUP * PAIR
FAR = 1e30

KIDS = {0: (2, 1), 2: (5, 3), 5: (8, 7, 4, 6)}
SLOTS = (0, 2, -2, 1, -1, 5, -5, 3, -3, 8, 7, -7, 4, -4, 6, -6)
SLOT = {d: s for s, d in enumerate(SLOTS)}
SLOT[-8] = SLOT[8]
UNITS = [(s, side) for s in range(8) for side in (0, 1)] + [(s, side) for side in (0, 1) for s in range(8, 16)]
UNIT = {unit: u for u, unit in enumerate(UNITS)}
REACH = 3
COUNT_SEM = {2: 0, -2: 1, 5: 2, -5: 3}
EDGES = {}
for parent, kids in KIDS.items():
    for kid in kids:
        for sign in (1, -1):
            EDGES[sign * kid] = sign * parent
EDGE = {d: e for e, d in enumerate(EDGES)}


def below(parent):
    sign = -1 if parent < 0 else 1
    kids = KIDS.get(abs(parent), ())
    if parent == 0:
        return [s * k for k in kids for s in (1, -1)]
    return [sign * k for k in kids]


ORDER = (2, 1, 3, 0)
HOPS = (2, 1, 3)
OFFSETS = [(dx, dy) for dy in ORDER for dx in ORDER]
PEERS = [o for o in OFFSETS if o != (0, 0)]
MATES = [(dx, dy, dc) for dx, dy in OFFSETS for dc in (0, 1) if (dx, dy, dc) != (0, 0, 0)]


def kernel(emb, ints, out_ref, log_ref, xz, cols, kern, acc, fold, mass, ni, cm, tsum, sg, send_x, recv_x, send_y, recv_y,
           sum_y, last_x, last_y, loc_sem, sent,
           e_recv, d_recv, c_recv, m_sem, r_recv, a_recv):
    z = lax.axis_index("dp")
    p = lax.axis_index("pair")
    core = lax.rem(p, 2)
    chip = p // 2
    x = lax.rem(chip, SIDE)
    y = chip // SIDE
    half = chip // 2

    def along(d):
        return (lax.rem(z + d + OWNERS, OWNERS), p)

    def place(dx, dy):
        return lax.rem(y + dy, SIDE) * SIDE + lax.rem(x + dx, SIDE)

    def peer(dx, dy):
        return (z, place(dx, dy) * 2 + core)

    other = (z, chip * 2 + 1 - core)

    barrier = pltpu.get_barrier_semaphore()
    for d in range(1, REACH + 1):
        for s in (1, -1):
            pl.semaphore_signal(barrier, 1, device_id=along(s * d), device_id_type=MESH)
    for dx, dy, dc in MATES:
        mate = (z, place(dx, dy) * 2 + lax.rem(core + dc, 2))
        pl.semaphore_signal(barrier, 1, device_id=mate, device_id_type=MESH)

    loads = [
        pltpu.make_async_copy(emb.at[chip, core], cols.at[pl.ds(0, SHARD)], loc_sem.at[0]),
        pltpu.make_async_copy(emb.at[chip, 1 - core], cols.at[pl.ds(SHARD, SHARD)], loc_sem.at[0]),
    ]
    for k in range(CHIPS):
        loads.append(pltpu.make_async_copy(emb.at[k, core], xz.at[pl.ds(k * SHARD, SHARD)], loc_sem.at[1]))
    for c in loads:
        c.start()

    sub8 = lax.broadcasted_iota(I32, (COUNT, 128), 0)
    lane8 = lax.broadcasted_iota(I32, (COUNT, 128), 1)
    sub128 = lax.broadcasted_iota(I32, (128, 128), 0)
    lane128 = lax.broadcasted_iota(I32, (128, 128), 1)
    spread = jnp.where(lane128 // COUNT == sub128, 1.0, 0.0).astype(BF16)
    wide = jnp.dot(ints[...].astype(BF16), spread, preferred_element_type=F32).astype(I32)
    near = sub8 == wide[2:3]
    for k in range(3, 6):
        near = jnp.logical_or(near, sub8 == wide[k:k + 1])
    far = wide[1:2] == lax.rem(lane8, COUNT)
    cm[0] = jnp.where(jnp.logical_and(near, far), 1.0, 0.0)
    pl.semaphore_wait(barrier, 2 * REACH + len(MATES))

    def span(d):
        return (0, 16) if d == 8 else (16, 16) if d == -8 else (0, SHARD)

    def held(s, side, r0=0, nr=SHARD):
        return cols.at[pl.ds(UNIT[s, side] * SHARD + r0, nr)]

    def rows_copy(d):
        parent = EDGES[d]
        r0, nr = span(d)
        if parent == 0:
            src = emb.at[chip, core, pl.ds(r0, nr)]
        else:
            src = held(SLOT[parent], 0, r0, nr)
        return pltpu.make_async_remote_copy(
            src_ref=src, dst_ref=held(SLOT[d], 0, r0, nr), send_sem=sent.at[0],
            recv_sem=e_recv.at[EDGE[d]], device_id=along(d - parent), device_id_type=MESH)

    def twin_copy(s):
        return pltpu.make_async_remote_copy(
            src_ref=held(s, 0), dst_ref=held(s, 1),
            send_sem=sent.at[1], recv_sem=d_recv.at[min(s // GROUP, 2)], device_id=other, device_id_type=MESH)

    def count_copy(d):
        parent = EDGES[d]
        return pltpu.make_async_remote_copy(
            src_ref=cm.at[SLOT[parent]], dst_ref=cm.at[SLOT[d]], send_sem=sent.at[2],
            recv_sem=c_recv.at[COUNT_SEM.get(d, 4)], device_id=along(d - parent), device_id_type=MESH)

    def rows_in(*ds):
        for d in ds:
            rows_copy(d).wait_recv()
            for k in below(d):
                rows_copy(k).start()
        for d in ds:
            if d != 8:
                twin_copy(SLOT[d]).start()

    def counts_in(*ds):
        for d in ds:
            count_copy(d).wait_recv()
            for k in below(d):
                if k != -8:
                    count_copy(k).start()

    def rest_in():
        come = cm.at[pl.ds(0, OWNERS - 1 - len(COUNT_SEM))]
        pltpu.make_async_copy(come, come, c_recv.at[4]).wait()

    for d in below(0):
        count_copy(d).start()
    for d in below(0):
        rows_copy(d).start()

    pltpu.make_async_copy(xz, xz, loc_sem.at[1]).wait()
    bs = ints[0:1]
    for k in range(ROWS // 128):
        v = xz[k * 128:(k + 1) * 128].astype(F32)
        n = jnp.sum(v * v, axis=1, keepdims=True)
        t = k * 128 + lax.broadcasted_iota(I32, (128, 128), 0)
        lane = lax.broadcasted_iota(I32, (128, 128), 1)
        size = jnp.sum(jnp.where(lane == z * COUNT + t // PAIR, bs, 0.0), axis=1, keepdims=True)
        inside = lax.rem(t // SHARD, 2) * PAIR + core * SHARD + lax.rem(t, SHARD)
        ni[k * 128:(k + 1) * 128] = n + jnp.where(inside.astype(F32) >= size, FAR, 0.0)

    lane1 = lax.broadcasted_iota(I32, (1, 128), 1)
    row32 = lax.broadcasted_iota(I32, (SHARD, 128), 0)
    inside32 = [(lax.rem(chip, 2) * PAIR + c * SHARD + row32).astype(F32) for c in (core, 1 - core)]

    def owner(d):
        return lax.rem(z - d + 2 * OWNERS, OWNERS)

    def far_norms(g):
        parts = []
        for u0 in range(g * 8, g * 8 + 8, 4):
            units = []
            for u in range(u0, u0 + 4):
                s, side = UNITS[u]
                v = cols[u * SHARD:(u + 1) * SHARD].astype(F32)
                n = jnp.sum(v * v, axis=1, keepdims=True)
                block = owner(SLOTS[s]) * COUNT + half
                size = jnp.sum(jnp.where(lane1 == block, bs, 0.0), axis=1, keepdims=True)
                units.append(n + jnp.where(inside32[side] >= size, FAR, 0.0))
            n = jnp.concatenate(units, axis=0)
            parts.append(jnp.sum(jnp.where(sub128 == lane128, n, 0.0), axis=0, keepdims=True))
        return jnp.concatenate(parts, axis=1)

    def near(g):
        if g == 0:
            both = cols.at[pl.ds(0, PAIR)]
            pltpu.make_async_copy(both, both, loc_sem.at[0]).wait()
        if g != 2:
            come = cols.at[pl.ds(0, (GROUP - 1, GROUP, 0, 2 * GROUP)[g] * SHARD)]
            pltpu.make_async_copy(come, come, d_recv.at[min(g, 2)]).wait()
        nj = far_norms(g)
        for r in range(0, ROWS, 256):
            dots = lax.dot_general(xz[r:r + 256], cols[g * COLS:(g + 1) * COLS], (((1,), (1,)), ((), ())),
                                   preferred_element_type=F32)
            n = ni[r:r + 256]
            dist = jnp.concatenate([n, n], axis=1) + nj - 2.0 * dots
            kern[r:r + 256, g * COLS:(g + 1) * COLS] = jnp.exp(-dist)

    counts_in(2, -2)
    rows_in(2, -2)
    rows_in(1, -1)
    counts_in(5, -5)
    rows_in(5, -5)
    rows_in(3, -3)
    rest_in()

    slot1 = lane1 // COUNT
    own1 = jnp.zeros((1, 128), I32)
    for s, d in enumerate(SLOTS):
        own1 = jnp.where(slot1 == s, owner(d), own1)
    own1 = own1 * COUNT + lax.rem(lane1, COUNT)
    perm = jnp.where(sub128 == own1, 1.0, 0.0).astype(BF16)
    pick = jnp.where(lane8 == z * COUNT + sub8, 1.0, 0.0).astype(BF16)
    there = cm[...].reshape(OWNERS * COUNT, 128).astype(BF16)
    pairs = jnp.dot(cm[0].astype(BF16), perm, preferred_element_type=F32) + lax.dot_general(
        pick, there, (((1,), (1,)), ((), ())), preferred_element_type=F32)
    tsum[2 * CHIPS - 1] = pairs
    for i, (dx, dy, dc) in enumerate(MATES):
        pltpu.make_async_remote_copy(
            src_ref=tsum.at[2 * CHIPS - 1], dst_ref=tsum.at[i], send_sem=m_sem.at[0], recv_sem=m_sem.at[1],
            device_id=(z, place(dx, dy) * 2 + lax.rem(core + dc, 2)), device_id_type=MESH).start()
    near(0)
    near(1)
    rows_in(8, -8)
    rows_in(7, -7)
    rows_in(4, -4)
    rows_in(6, -6)
    near(2)
    mates = tsum.at[pl.ds(0, len(MATES))]
    pltpu.make_async_copy(mates, mates, m_sem.at[1]).wait()
    total = tsum[2 * CHIPS - 1]
    for i in range(len(MATES)):
        total = total + tsum[i]
    times = [jnp.sum(jnp.where(lane8 == s * COUNT + half, total, 0.0), axis=1, keepdims=True) for s in range(OWNERS)]
    for u in range(0, 2 * OWNERS, 4):
        four = [times[UNITS[u + k][0]] for k in range(4)]
        low = jnp.where(lane8 < SHARD, four[0], four[1])
        high = jnp.where(lane8 < 3 * SHARD, four[2], four[3])
        sg[:, u * SHARD:(u + 4) * SHARD] = jnp.where(lane8 < PAIR, low, high)

    def sums(row, c0, c1):
        k = kern[pl.ds(row * 128, 128), c0:c1]
        s0 = jnp.broadcast_to(sg[pl.ds(row * 2, 1), c0:c1], (PAIR, c1 - c0))
        s1 = jnp.broadcast_to(sg[pl.ds(row * 2 + 1, 1), c0:c1], (PAIR, c1 - c0))
        s = jnp.concatenate([s0, s1], axis=0)
        w = s * k.astype(BF16).astype(F32)
        hi = w.astype(BF16)
        lo = (w - hi.astype(F32)).astype(BF16)
        far = cols[c0:c1]
        t = jnp.dot(hi, far, preferred_element_type=F32) + jnp.dot(lo, far, preferred_element_type=F32)
        m = s * k
        return t, sum(m[:, 128 * h:128 * (h + 1)] for h in range((c1 - c0) // 128))

    acc[ORDER[0]], fold[...] = sums(lax.rem(y + ORDER[0], SIDE), 0, 3 * COLS)
    near(3)

    lane32 = lax.broadcasted_iota(I32, (SHARD, 128), 1)
    sub32 = lax.broadcasted_iota(I32, (SHARD, 128), 0)

    def spot(step):
        return pl.ds(lax.rem(x + step, SIDE) * SHARD, SHARD)

    def send_to(src, dst, sem, dx, dy, kind):
        pltpu.make_async_remote_copy(src_ref=src, dst_ref=dst, send_sem=sent.at[kind], recv_sem=sem,
                                     device_id=peer(dx, dy), device_id_type=MESH).start()

    i = 0
    for dy in ORDER:
        if dy == ORDER[0]:
            t, m = sums(lax.rem(y + dy, SIDE), 3 * COLS, 4 * COLS)
            t, m = t + acc[dy], m + fold[...]
        else:
            t, m = sums(lax.rem(y + dy, SIDE), 0, 4 * COLS)
        acc[dy] = t
        if dy:
            send_y[dy - 1] = t[:, CUT:].astype(BF16)
            send_to(send_y.at[dy - 1], recv_y.at[dy - 1], r_recv.at[4], 0, dy, 4)
        for dx in HOPS:
            send_x[dx - 1, dy] = acc[dy, spot(dx), :CUT].astype(BF16)
            send_to(send_x.at[dx - 1, dy], recv_x.at[dx - 1, dy], r_recv.at[dy], dx, 0, 3)
        m = jnp.sum(m, axis=1, keepdims=True)
        mass[dy] = jnp.sum(jnp.where(sub128 == lane128, m, 0.0), axis=0, keepdims=True)
        for dx in ORDER:
            if (dx, dy) != (0, 0):
                send_to(mass.at[dy], mass.at[SIDE + i], a_recv.at[0], dx, dy, 5)
                i += 1

    def come(ref, sem):
        pltpu.make_async_copy(ref, ref, sem).wait()

    def first_x(dy):
        come(recv_x.at[:, dy], r_recv.at[dy])
        v = acc[dy, spot(0), :CUT]
        for k in range(SIDE - 1):
            v = v + recv_x[k, dy].astype(F32)
        return v

    def along_y(dy):
        last_y[dy - 1] = first_x(dy)
        send_to(last_y.at[dy - 1], last_y.at[SIDE - 2 + dy], r_recv.at[6], 0, dy, 7)

    along_y(2)
    along_y(1)
    come(recv_y, r_recv.at[4])
    v = acc[0, :, CUT:]
    for k in range(SIDE - 1):
        v = v + recv_y[k].astype(F32)
    sum_y[...] = v
    for dx in HOPS:
        last_x[dx - 1] = sum_y[spot(dx)]
        send_to(last_x.at[dx - 1], last_x.at[SIDE - 2 + dx], r_recv.at[5], dx, 0, 6)
    along_y(3)
    v = first_x(0)
    a = mass[0]
    got = mass.at[pl.ds(SIDE, len(PEERS))]
    come(got, a_recv.at[0])
    for k in range(len(PEERS)):
        a = a + mass[SIDE + k]
    m = jnp.sum(jnp.where(lane32 == x * SHARD + sub32, a, 0.0), axis=1, keepdims=True)
    m = jnp.log(1.0 + m)
    log_ref[...] = jnp.sum(jnp.where(sub32 == lane32, m, 0.0), axis=0, keepdims=True)
    w = sum_y[spot(0)]
    there_x = last_x.at[pl.ds(SIDE - 1, SIDE - 1)]
    there_y = last_y.at[pl.ds(SIDE - 1, SIDE - 1)]
    come(there_x, r_recv.at[5])
    for k in range(SIDE - 1):
        w = w + last_x[SIDE - 1 + k]
    out_ref[:, CUT:] = w
    come(there_y, r_recv.at[6])
    for k in range(SIDE - 1):
        v = v + last_y[SIDE - 1 + k]
    out_ref[:, :CUT] = v
    shards = cols.at[pl.ds(0, (OWNERS - 1) * SHARD)]
    counted = cm.at[pl.ds(0, OWNERS - 1)]
    for what, sem in ((shards, sent.at[0]), (shards, sent.at[1]), (counted, sent.at[2]), (recv_x, sent.at[3]),
                      (recv_y, sent.at[4]), (got, sent.at[5]), (there_x, sent.at[6]), (there_y, sent.at[7]),
                      (mates, m_sem.at[0])):
        come(what, sem)


def body(embeddings, block_sizes, fetch_blocks, partners):
    hbm = pl.BlockSpec(memory_space=pltpu.HBM)
    vmem = pl.BlockSpec(memory_space=pltpu.VMEM)
    dma = pltpu.SemaphoreType.DMA
    edges = len(EDGES)
    room = ((0, 0), (0, 128 - OWNERS))
    ints = jnp.concatenate([
        block_sizes.reshape(1, 128),
        jnp.pad(fetch_blocks.reshape(1, OWNERS), room),
        jnp.pad(jnp.swapaxes(partners, 2, 3).reshape(4, OWNERS), room),
        jnp.zeros((2, 128), I32),
    ]).astype(F32)
    out, logs = pl.pallas_call(
        kernel,
        out_shape=(jax.ShapeDtypeStruct((SHARD, WIDTH), F32), jax.ShapeDtypeStruct((1, 128), F32)),
        in_specs=[hbm, vmem],
        out_specs=(vmem, vmem),
        scratch_shapes=[
            pltpu.VMEM((ROWS, WIDTH), BF16),
            pltpu.VMEM((OWNERS * PAIR, WIDTH), BF16),
            pltpu.VMEM((ROWS, OWNERS * PAIR), F32),
            pltpu.VMEM((SIDE, 128, WIDTH), F32),
            pltpu.VMEM((128, 128), F32),
            pltpu.VMEM((SIDE + len(PEERS), 1, 128), F32),
            pltpu.VMEM((ROWS, 128), F32),
            pltpu.VMEM((OWNERS, COUNT, 128), F32),
            pltpu.VMEM((2 * CHIPS, COUNT, 128), F32),
            pltpu.VMEM((COUNT, OWNERS * PAIR), F32),
            pltpu.VMEM((SIDE - 1, SIDE, SHARD, CUT), BF16),
            pltpu.VMEM((SIDE - 1, SIDE, SHARD, CUT), BF16),
            pltpu.VMEM((SIDE - 1, 128, WIDTH - CUT), BF16),
            pltpu.VMEM((SIDE - 1, 128, WIDTH - CUT), BF16),
            pltpu.VMEM((128, WIDTH - CUT), F32),
            pltpu.VMEM((2 * (SIDE - 1), SHARD, WIDTH - CUT), F32),
            pltpu.VMEM((2 * (SIDE - 1), SHARD, CUT), F32),
            dma((2,)),
            dma((8,)),
            dma((edges,)),
            dma((3,)),
            dma((len(COUNT_SEM) + 1,)),
            dma((2,)),
            dma((7,)),
            dma((1,)),
        ],
        compiler_params=pltpu.CompilerParams(collective_id=0, has_side_effects=True, vmem_limit_bytes=53 << 20),
        cost_estimate=pl.CostEstimate(flops=3 * 2 * 512 * 1024 * 768, bytes_accessed=4 << 20, transcendentals=512 * 1024),
    )(embeddings.reshape(CHIPS, 2, SHARD, WIDTH), ints)
    return out, logs[0, :SHARD]


def solution(mesh):
    return jax.shard_map(
        body,
        mesh=mesh,
        in_specs=(P("dp", None), P(), P("dp", "pair", None), P("dp", "pair", None, None)),
        out_specs=(P(("dp", "pair"), None), P(("dp", "pair"))),
        check_vma=False,
    )
```

```python
import jax
import jax.numpy as jnp
from jax import lax
from jax.experimental import pallas as pl
from jax.experimental.pallas import tpu as pltpu
from jax.sharding import PartitionSpec as P

MESH = pl.DeviceIdType.MESH
F32, BF16, I32 = jnp.float32, jnp.bfloat16, jnp.int32

OWNERS, COUNT, DEPTH, WIDTH = 16, 8, 128, 768
SIDE = 4
CHIPS = SIDE * SIDE
SHARD = 32
ROWS = CHIPS * SHARD
PAIR = 2 * SHARD
GROUP = 4
CUT = 640
COLS = GROUP * PAIR
FAR = 1e30

KIDS = {0: (2, 1), 2: (5, 3), 5: (8, 7, 4, 6)}
SLOTS = (0, 2, -2, 1, -1, 5, -5, 3, -3, 8, 7, -7, 4, -4, 6, -6)
SLOT = {d: s for s, d in enumerate(SLOTS)}
SLOT[-8] = SLOT[8]
UNITS = [(s, side) for s in range(8) for side in (0, 1)] + [(s, side) for side in (0, 1) for s in range(8, 16)]
UNIT = {unit: u for u, unit in enumerate(UNITS)}
REACH = 3
COUNT_SEM = {2: 0, -2: 1, 5: 2, -5: 3}
EDGES = {}
for parent, kids in KIDS.items():
    for kid in kids:
        for sign in (1, -1):
            EDGES[sign * kid] = sign * parent
EDGE = {d: e for e, d in enumerate(EDGES)}


def below(parent):
    sign = -1 if parent < 0 else 1
    kids = KIDS.get(abs(parent), ())
    if parent == 0:
        return [s * k for k in kids for s in (1, -1)]
    return [sign * k for k in kids]


ORDER = (2, 1, 3, 0)
HOPS = (2, 1, 3)
OFFSETS = [(dx, dy) for dy in ORDER for dx in ORDER]
PEERS = [o for o in OFFSETS if o != (0, 0)]
MATES = [(dx, dy, dc) for dx, dy in OFFSETS for dc in (0, 1) if (dx, dy, dc) != (0, 0, 0)]


def kernel(emb, ints, out_ref, log_ref, xz, cols, kern, acc, fold, mass, ni, cm, tsum, sg, send_u, recv_u, send_v, recv_v,
           sum_v, last_u, last_v, loc_sem, sent,
           e_recv, d_recv, c_recv, m_sem, r_recv, a_recv):
    z = lax.axis_index("dp")
    p = lax.axis_index("pair")
    core = lax.rem(p, 2)
    chip = p // 2
    x = lax.rem(chip, SIDE)
    y = chip // SIDE
    half = chip // 2

    def along(d):
        return (lax.rem(z + d + OWNERS, OWNERS), p)

    def place(dx, dy):
        return lax.rem(y + dy, SIDE) * SIDE + lax.rem(x + dx, SIDE)

    own_u = x + core * (y - x)
    own_v = y + core * (x - y)

    def peer(du, dv):
        return (z, place(du + core * (dv - du), dv + core * (du - dv)) * 2 + core)

    other = (z, chip * 2 + 1 - core)

    barrier = pltpu.get_barrier_semaphore()
    for d in range(1, REACH + 1):
        for s in (1, -1):
            pl.semaphore_signal(barrier, 1, device_id=along(s * d), device_id_type=MESH)
    for dx, dy, dc in MATES:
        mate = (z, place(dx, dy) * 2 + lax.rem(core + dc, 2))
        pl.semaphore_signal(barrier, 1, device_id=mate, device_id_type=MESH)

    loads = [
        pltpu.make_async_copy(emb.at[chip, core], cols.at[pl.ds(0, SHARD)], loc_sem.at[0]),
        pltpu.make_async_copy(emb.at[chip, 1 - core], cols.at[pl.ds(SHARD, SHARD)], loc_sem.at[0]),
    ]
    for k in range(CHIPS):
        other_way = k % SIDE * SIDE + k // SIDE
        loads.append(pltpu.make_async_copy(emb.at[k + core * (other_way - k), core], xz.at[pl.ds(k * SHARD, SHARD)], loc_sem.at[1]))
    for c in loads:
        c.start()

    sub8 = lax.broadcasted_iota(I32, (COUNT, 128), 0)
    lane8 = lax.broadcasted_iota(I32, (COUNT, 128), 1)
    sub128 = lax.broadcasted_iota(I32, (128, 128), 0)
    lane128 = lax.broadcasted_iota(I32, (128, 128), 1)
    spread = jnp.where(lane128 // COUNT == sub128, 1.0, 0.0).astype(BF16)
    wide = jnp.dot(ints[...].astype(BF16), spread, preferred_element_type=F32).astype(I32)
    near = sub8 == wide[2:3]
    for k in range(3, 6):
        near = jnp.logical_or(near, sub8 == wide[k:k + 1])
    far = wide[1:2] == lax.rem(lane8, COUNT)
    cm[0] = jnp.where(jnp.logical_and(near, far), 1.0, 0.0)
    pl.semaphore_wait(barrier, 2 * REACH + len(MATES))

    def span(d):
        return (0, 16) if d == 8 else (16, 16) if d == -8 else (0, SHARD)

    def held(s, side, r0=0, nr=SHARD):
        return cols.at[pl.ds(UNIT[s, side] * SHARD + r0, nr)]

    def rows_copy(d):
        parent = EDGES[d]
        r0, nr = span(d)
        if parent == 0:
            src = emb.at[chip, core, pl.ds(r0, nr)]
        else:
            src = held(SLOT[parent], 0, r0, nr)
        return pltpu.make_async_remote_copy(
            src_ref=src, dst_ref=held(SLOT[d], 0, r0, nr), send_sem=sent.at[0],
            recv_sem=e_recv.at[EDGE[d]], device_id=along(d - parent), device_id_type=MESH)

    def twin_copy(s):
        return pltpu.make_async_remote_copy(
            src_ref=held(s, 0), dst_ref=held(s, 1),
            send_sem=sent.at[1], recv_sem=d_recv.at[min(s // GROUP, 2)], device_id=other, device_id_type=MESH)

    def count_copy(d):
        parent = EDGES[d]
        return pltpu.make_async_remote_copy(
            src_ref=cm.at[SLOT[parent]], dst_ref=cm.at[SLOT[d]], send_sem=sent.at[2],
            recv_sem=c_recv.at[COUNT_SEM.get(d, 4)], device_id=along(d - parent), device_id_type=MESH)

    def rows_in(*ds):
        for d in ds:
            rows_copy(d).wait_recv()
            for k in below(d):
                rows_copy(k).start()
        for d in ds:
            if d != 8:
                twin_copy(SLOT[d]).start()

    def counts_in(*ds):
        for d in ds:
            count_copy(d).wait_recv()
            for k in below(d):
                if k != -8:
                    count_copy(k).start()

    def rest_in():
        come = cm.at[pl.ds(0, OWNERS - 1 - len(COUNT_SEM))]
        pltpu.make_async_copy(come, come, c_recv.at[4]).wait()

    for d in below(0):
        count_copy(d).start()
    for d in below(0):
        rows_copy(d).start()

    pltpu.make_async_copy(xz, xz, loc_sem.at[1]).wait()
    bs = ints[0:1]
    for k in range(ROWS // 128):
        v = xz[k * 128:(k + 1) * 128].astype(F32)
        n = jnp.sum(v * v, axis=1, keepdims=True)
        at = k * SIDE + sub128 // SHARD
        at = at + core * (lax.rem(at, SIDE) * SIDE + at // SIDE - at)
        lane = lax.broadcasted_iota(I32, (128, 128), 1)
        size = jnp.sum(jnp.where(lane == z * COUNT + at // 2, bs, 0.0), axis=1, keepdims=True)
        inside = lax.rem(at, 2) * PAIR + core * SHARD + lax.rem(sub128, SHARD)
        ni[k * 128:(k + 1) * 128] = n + jnp.where(inside.astype(F32) >= size, FAR, 0.0)

    lane1 = lax.broadcasted_iota(I32, (1, 128), 1)
    row32 = lax.broadcasted_iota(I32, (SHARD, 128), 0)
    inside32 = [(lax.rem(chip, 2) * PAIR + c * SHARD + row32).astype(F32) for c in (core, 1 - core)]

    def owner(d):
        return lax.rem(z - d + 2 * OWNERS, OWNERS)

    def far_norms(g):
        parts = []
        for u0 in range(g * 8, g * 8 + 8, 4):
            units = []
            for u in range(u0, u0 + 4):
                s, side = UNITS[u]
                v = cols[u * SHARD:(u + 1) * SHARD].astype(F32)
                n = jnp.sum(v * v, axis=1, keepdims=True)
                block = owner(SLOTS[s]) * COUNT + half
                size = jnp.sum(jnp.where(lane1 == block, bs, 0.0), axis=1, keepdims=True)
                units.append(n + jnp.where(inside32[side] >= size, FAR, 0.0))
            n = jnp.concatenate(units, axis=0)
            parts.append(jnp.sum(jnp.where(sub128 == lane128, n, 0.0), axis=0, keepdims=True))
        return jnp.concatenate(parts, axis=1)

    def near(g):
        if g == 0:
            both = cols.at[pl.ds(0, PAIR)]
            pltpu.make_async_copy(both, both, loc_sem.at[0]).wait()
        if g != 2:
            come = cols.at[pl.ds(0, (GROUP - 1, GROUP, 0, 2 * GROUP)[g] * SHARD)]
            pltpu.make_async_copy(come, come, d_recv.at[min(g, 2)]).wait()
        nj = far_norms(g)
        for r in range(0, ROWS, 256):
            dots = lax.dot_general(xz[r:r + 256], cols[g * COLS:(g + 1) * COLS], (((1,), (1,)), ((), ())),
                                   preferred_element_type=F32)
            n = ni[r:r + 256]
            dist = jnp.concatenate([n, n], axis=1) + nj - 2.0 * dots
            kern[r:r + 256, g * COLS:(g + 1) * COLS] = jnp.exp(-dist)

    counts_in(2, -2)
    rows_in(2, -2)
    rows_in(1, -1)
    counts_in(5, -5)
    rows_in(5, -5)
    rows_in(3, -3)
    rest_in()

    slot1 = lane1 // COUNT
    own1 = jnp.zeros((1, 128), I32)
    for s, d in enumerate(SLOTS):
        own1 = jnp.where(slot1 == s, owner(d), own1)
    own1 = own1 * COUNT + lax.rem(lane1, COUNT)
    perm = jnp.where(sub128 == own1, 1.0, 0.0).astype(BF16)
    pick = jnp.where(lane8 == z * COUNT + sub8, 1.0, 0.0).astype(BF16)
    there = cm[...].reshape(OWNERS * COUNT, 128).astype(BF16)
    pairs = jnp.dot(cm[0].astype(BF16), perm, preferred_element_type=F32) + lax.dot_general(
        pick, there, (((1,), (1,)), ((), ())), preferred_element_type=F32)
    tsum[2 * CHIPS - 1] = pairs
    for i, (dx, dy, dc) in enumerate(MATES):
        pltpu.make_async_remote_copy(
            src_ref=tsum.at[2 * CHIPS - 1], dst_ref=tsum.at[i], send_sem=m_sem.at[0], recv_sem=m_sem.at[1],
            device_id=(z, place(dx, dy) * 2 + lax.rem(core + dc, 2)), device_id_type=MESH).start()
    near(0)
    near(1)
    rows_in(8, -8)
    rows_in(7, -7)
    rows_in(4, -4)
    rows_in(6, -6)
    near(2)
    mates = tsum.at[pl.ds(0, len(MATES))]
    pltpu.make_async_copy(mates, mates, m_sem.at[1]).wait()
    total = tsum[2 * CHIPS - 1]
    for i in range(len(MATES)):
        total = total + tsum[i]
    times = [jnp.sum(jnp.where(lane8 == s * COUNT + half, total, 0.0), axis=1, keepdims=True) for s in range(OWNERS)]
    for u in range(0, 2 * OWNERS, 4):
        four = [times[UNITS[u + k][0]] for k in range(4)]
        low = jnp.where(lane8 < SHARD, four[0], four[1])
        high = jnp.where(lane8 < 3 * SHARD, four[2], four[3])
        sg[:, u * SHARD:(u + 4) * SHARD] = jnp.where(lane8 < PAIR, low, high)

    def sums(row, c0, c1):
        k = kern[pl.ds(row * 128, 128), c0:c1]
        s = []
        for h in range(SIDE):
            block = (row * SIDE + h + core * (h * SIDE + row - row * SIDE - h)) // 2
            s.append(jnp.broadcast_to(sg[pl.ds(block, 1), c0:c1], (SHARD, c1 - c0)))
        s = jnp.concatenate(s, axis=0)
        w = s * k.astype(BF16).astype(F32)
        hi = w.astype(BF16)
        lo = (w - hi.astype(F32)).astype(BF16)
        far = cols[c0:c1]
        t = jnp.dot(hi, far, preferred_element_type=F32) + jnp.dot(lo, far, preferred_element_type=F32)
        m = s * k
        return t, sum(m[:, 128 * h:128 * (h + 1)] for h in range((c1 - c0) // 128))

    acc[ORDER[0]], fold[...] = sums(lax.rem(own_v + ORDER[0], SIDE), 0, 3 * COLS)
    near(3)

    lane32 = lax.broadcasted_iota(I32, (SHARD, 128), 1)
    sub32 = lax.broadcasted_iota(I32, (SHARD, 128), 0)

    def spot(step):
        return pl.ds(lax.rem(own_u + step, SIDE) * SHARD, SHARD)

    def send_to(src, dst, sem, du, dv, kind):
        pltpu.make_async_remote_copy(src_ref=src, dst_ref=dst, send_sem=sent.at[kind], recv_sem=sem,
                                     device_id=peer(du, dv), device_id_type=MESH).start()

    i = 0
    for dv in ORDER:
        if dv == ORDER[0]:
            t, m = sums(lax.rem(own_v + dv, SIDE), 3 * COLS, 4 * COLS)
            t, m = t + acc[dv], m + fold[...]
        else:
            t, m = sums(lax.rem(own_v + dv, SIDE), 0, 4 * COLS)
        acc[dv] = t
        if dv:
            send_v[dv - 1] = t[:, CUT:].astype(BF16)
            send_to(send_v.at[dv - 1], recv_v.at[dv - 1], r_recv.at[4], 0, dv, 4)
        for du in HOPS:
            send_u[du - 1, dv] = acc[dv, spot(du), :CUT].astype(BF16)
            send_to(send_u.at[du - 1, dv], recv_u.at[du - 1, dv], r_recv.at[dv], du, 0, 3)
        m = jnp.sum(m, axis=1, keepdims=True)
        mass[dv] = jnp.sum(jnp.where(sub128 == lane128, m, 0.0), axis=0, keepdims=True)
        for du in ORDER:
            if (du, dv) != (0, 0):
                send_to(mass.at[dv], mass.at[SIDE + i], a_recv.at[0], du, dv, 5)
                i += 1

    def come(ref, sem):
        pltpu.make_async_copy(ref, ref, sem).wait()

    def first_u(dv):
        come(recv_u.at[:, dv], r_recv.at[dv])
        r = acc[dv, spot(0), :CUT]
        for k in range(SIDE - 1):
            r = r + recv_u[k, dv].astype(F32)
        return r

    def along_v(dv):
        last_v[dv - 1] = first_u(dv)
        send_to(last_v.at[dv - 1], last_v.at[SIDE - 2 + dv], r_recv.at[6], 0, dv, 7)

    along_v(2)
    along_v(1)
    come(recv_v, r_recv.at[4])
    r = acc[0, :, CUT:]
    for k in range(SIDE - 1):
        r = r + recv_v[k].astype(F32)
    sum_v[...] = r
    for du in HOPS:
        last_u[du - 1] = sum_v[spot(du)]
        send_to(last_u.at[du - 1], last_u.at[SIDE - 2 + du], r_recv.at[5], du, 0, 6)
    along_v(3)
    r = first_u(0)
    a = mass[0]
    got = mass.at[pl.ds(SIDE, len(PEERS))]
    come(got, a_recv.at[0])
    for k in range(len(PEERS)):
        a = a + mass[SIDE + k]
    m = jnp.sum(jnp.where(lane32 == own_u * SHARD + sub32, a, 0.0), axis=1, keepdims=True)
    m = jnp.log(1.0 + m)
    log_ref[...] = jnp.sum(jnp.where(sub32 == lane32, m, 0.0), axis=0, keepdims=True)
    w = sum_v[spot(0)]
    there_u = last_u.at[pl.ds(SIDE - 1, SIDE - 1)]
    there_v = last_v.at[pl.ds(SIDE - 1, SIDE - 1)]
    come(there_u, r_recv.at[5])
    for k in range(SIDE - 1):
        w = w + last_u[SIDE - 1 + k]
    out_ref[:, CUT:] = w
    come(there_v, r_recv.at[6])
    for k in range(SIDE - 1):
        r = r + last_v[SIDE - 1 + k]
    out_ref[:, :CUT] = r
    shards = cols.at[pl.ds(0, (OWNERS - 1) * SHARD)]
    counted = cm.at[pl.ds(0, OWNERS - 1)]
    for what, sem in ((shards, sent.at[0]), (shards, sent.at[1]), (counted, sent.at[2]), (recv_u, sent.at[3]),
                      (recv_v, sent.at[4]), (got, sent.at[5]), (there_u, sent.at[6]), (there_v, sent.at[7]),
                      (mates, m_sem.at[0])):
        come(what, sem)


def body(embeddings, block_sizes, fetch_blocks, partners):
    hbm = pl.BlockSpec(memory_space=pltpu.HBM)
    vmem = pl.BlockSpec(memory_space=pltpu.VMEM)
    dma = pltpu.SemaphoreType.DMA
    edges = len(EDGES)
    room = ((0, 0), (0, 128 - OWNERS))
    ints = jnp.concatenate([
        block_sizes.reshape(1, 128),
        jnp.pad(fetch_blocks.reshape(1, OWNERS), room),
        jnp.pad(jnp.swapaxes(partners, 2, 3).reshape(4, OWNERS), room),
    ]).astype(F32)
    out, logs = pl.pallas_call(
        kernel,
        out_shape=(jax.ShapeDtypeStruct((SHARD, WIDTH), F32), jax.ShapeDtypeStruct((1, 128), F32)),
        in_specs=[hbm, vmem],
        out_specs=(vmem, vmem),
        scratch_shapes=[
            pltpu.VMEM((ROWS, WIDTH), BF16),
            pltpu.VMEM((OWNERS * PAIR, WIDTH), BF16),
            pltpu.VMEM((ROWS, OWNERS * PAIR), F32),
            pltpu.VMEM((SIDE, 128, WIDTH), F32),
            pltpu.VMEM((128, 128), F32),
            pltpu.VMEM((SIDE + len(PEERS), 1, 128), F32),
            pltpu.VMEM((ROWS, 128), F32),
            pltpu.VMEM((OWNERS, COUNT, 128), F32),
            pltpu.VMEM((2 * CHIPS, COUNT, 128), F32),
            pltpu.VMEM((COUNT, OWNERS * PAIR), F32),
            pltpu.VMEM((SIDE - 1, SIDE, SHARD, CUT), BF16),
            pltpu.VMEM((SIDE - 1, SIDE, SHARD, CUT), BF16),
            pltpu.VMEM((SIDE - 1, 128, WIDTH - CUT), BF16),
            pltpu.VMEM((SIDE - 1, 128, WIDTH - CUT), BF16),
            pltpu.VMEM((128, WIDTH - CUT), F32),
            pltpu.VMEM((2 * (SIDE - 1), SHARD, WIDTH - CUT), F32),
            pltpu.VMEM((2 * (SIDE - 1), SHARD, CUT), F32),
            dma((2,)),
            dma((8,)),
            dma((edges,)),
            dma((3,)),
            dma((len(COUNT_SEM) + 1,)),
            dma((2,)),
            dma((7,)),
            dma((1,)),
        ],
        compiler_params=pltpu.CompilerParams(collective_id=0, has_side_effects=True, vmem_limit_bytes=53 << 20),
        cost_estimate=pl.CostEstimate(flops=3 * 2 * 512 * 1024 * 768, bytes_accessed=4 << 20, transcendentals=512 * 1024),
    )(embeddings.reshape(CHIPS, 2, SHARD, WIDTH), ints)
    return out, logs[0, :SHARD]


def solution(mesh):
    return jax.shard_map(
        body,
        mesh=mesh,
        in_specs=(P("dp", None), P(), P("dp", "pair", None), P("dp", "pair", None, None)),
        out_specs=(P(("dp", "pair"), None), P(("dp", "pair"))),
        check_vma=False,
    )
```

```python
import jax
import jax.numpy as jnp
from jax import lax
from jax.experimental import pallas as pl
from jax.experimental.pallas import tpu as pltpu
from jax.sharding import PartitionSpec as P

MESH = pl.DeviceIdType.MESH
F32, BF16, I32 = jnp.float32, jnp.bfloat16, jnp.int32

OWNERS, COUNT, DEPTH, WIDTH = 16, 8, 128, 768
SIDE = 4
CHIPS = SIDE * SIDE
SHARD = 32
ROWS = CHIPS * SHARD
PAIR = 2 * SHARD
GROUP = 4
CUT = 640
COLS = GROUP * PAIR
FAR = 1e30

KIDS = {0: (2, 1), 2: (5, 3), 5: (7, 8, 6, 4)}
SLOTS = (0, 2, -2, 1, -1, 5, -5, 3, -3, 8, 7, -7, 4, -4, 6, -6)
SLOT = {d: s for s, d in enumerate(SLOTS)}
SLOT[-8] = SLOT[8]
UNITS = [(s, side) for s in range(8) for side in (0, 1)] + [(s, side) for side in (0, 1) for s in range(8, 16)]
UNIT = {unit: u for u, unit in enumerate(UNITS)}
REACH = 3
COUNT_SEM = {2: 0, -2: 1, 5: 2, -5: 3}
EDGES = {}
for parent, kids in KIDS.items():
    for kid in kids:
        for sign in (1, -1):
            EDGES[sign * kid] = sign * parent
EDGE = {d: e for e, d in enumerate(EDGES)}


def below(parent):
    sign = -1 if parent < 0 else 1
    kids = KIDS.get(abs(parent), ())
    if parent == 0:
        return [s * k for k in kids for s in (1, -1)]
    return [sign * k for k in kids]


ORDER = (2, 1, 3, 0)
HOPS = (2, 1, 3)
OFFSETS = [(dx, dy) for dy in ORDER for dx in ORDER]
PEERS = [o for o in OFFSETS if o != (0, 0)]
MATES = [(dx, dy, dc) for dx, dy in OFFSETS for dc in (0, 1) if (dx, dy, dc) != (0, 0, 0)]


def kernel(emb, ints, out_ref, log_ref, xz, cols, kern, acc, fold, mass, ni, cm, tsum, sg, send_u, recv_u, send_v, recv_v,
           sum_v, last_u, last_v, loc_sem, sent,
           e_recv, d_recv, c_recv, m_sem, r_recv, a_recv):
    z = lax.axis_index("dp")
    p = lax.axis_index("pair")
    core = lax.rem(p, 2)
    chip = p // 2
    x = lax.rem(chip, SIDE)
    y = chip // SIDE
    half = chip // 2

    def along(d):
        return (lax.rem(z + d + OWNERS, OWNERS), p)

    def place(dx, dy):
        return lax.rem(y + dy, SIDE) * SIDE + lax.rem(x + dx, SIDE)

    own_u = x + core * (y - x)
    own_v = y + core * (x - y)

    def peer(du, dv):
        return (z, place(du + core * (dv - du), dv + core * (du - dv)) * 2 + core)

    other = (z, chip * 2 + 1 - core)

    barrier = pltpu.get_barrier_semaphore()
    for d in range(1, REACH + 1):
        for s in (1, -1):
            pl.semaphore_signal(barrier, 1, device_id=along(s * d), device_id_type=MESH)
    for dx, dy, dc in MATES:
        mate = (z, place(dx, dy) * 2 + lax.rem(core + dc, 2))
        pl.semaphore_signal(barrier, 1, device_id=mate, device_id_type=MESH)

    loads = [
        pltpu.make_async_copy(emb.at[chip, core], cols.at[pl.ds(0, SHARD)], loc_sem.at[0]),
        pltpu.make_async_copy(emb.at[chip, 1 - core], cols.at[pl.ds(SHARD, SHARD)], loc_sem.at[0]),
    ]
    for k in range(CHIPS):
        other_way = k % SIDE * SIDE + k // SIDE
        loads.append(pltpu.make_async_copy(emb.at[k + core * (other_way - k), core], xz.at[pl.ds(k * SHARD, SHARD)], loc_sem.at[1]))
    for c in loads:
        c.start()

    sub8 = lax.broadcasted_iota(I32, (COUNT, 128), 0)
    lane8 = lax.broadcasted_iota(I32, (COUNT, 128), 1)
    sub128 = lax.broadcasted_iota(I32, (128, 128), 0)
    lane128 = lax.broadcasted_iota(I32, (128, 128), 1)
    spread = jnp.where(lane128 // COUNT == sub128, 1.0, 0.0).astype(BF16)
    wide = jnp.dot(ints[...].astype(BF16), spread, preferred_element_type=F32).astype(I32)
    near = sub8 == wide[2:3]
    for k in range(3, 6):
        near = jnp.logical_or(near, sub8 == wide[k:k + 1])
    far = wide[1:2] == lax.rem(lane8, COUNT)
    cm[0] = jnp.where(jnp.logical_and(near, far), 1.0, 0.0)
    pl.semaphore_wait(barrier, 2 * REACH + len(MATES))

    def span(d):
        return (0, 16) if d == 8 else (16, 16) if d == -8 else (0, SHARD)

    def held(s, side, r0=0, nr=SHARD):
        return cols.at[pl.ds(UNIT[s, side] * SHARD + r0, nr)]

    def rows_copy(d):
        parent = EDGES[d]
        r0, nr = span(d)
        if parent == 0:
            src = emb.at[chip, core, pl.ds(r0, nr)]
        else:
            src = held(SLOT[parent], 0, r0, nr)
        return pltpu.make_async_remote_copy(
            src_ref=src, dst_ref=held(SLOT[d], 0, r0, nr), send_sem=sent.at[0],
            recv_sem=e_recv.at[EDGE[d]], device_id=along(d - parent), device_id_type=MESH)

    def twin_copy(s):
        return pltpu.make_async_remote_copy(
            src_ref=held(s, 0), dst_ref=held(s, 1),
            send_sem=sent.at[1], recv_sem=d_recv.at[min(s // GROUP, 2)], device_id=other, device_id_type=MESH)

    def count_copy(d):
        parent = EDGES[d]
        return pltpu.make_async_remote_copy(
            src_ref=cm.at[SLOT[parent]], dst_ref=cm.at[SLOT[d]], send_sem=sent.at[2],
            recv_sem=c_recv.at[COUNT_SEM.get(d, 4)], device_id=along(d - parent), device_id_type=MESH)

    def rows_in(*ds):
        for d in ds:
            rows_copy(d).wait_recv()
            for k in below(d):
                rows_copy(k).start()
        for d in ds:
            if d != 8:
                twin_copy(SLOT[d]).start()

    def counts_in(*ds):
        for d in ds:
            count_copy(d).wait_recv()
            for k in below(d):
                if k != -8:
                    count_copy(k).start()

    def rest_in():
        come = cm.at[pl.ds(0, OWNERS - 1 - len(COUNT_SEM))]
        pltpu.make_async_copy(come, come, c_recv.at[4]).wait()

    for d in below(0):
        count_copy(d).start()
    for d in below(0):
        rows_copy(d).start()

    pltpu.make_async_copy(xz, xz, loc_sem.at[1]).wait()
    bs = ints[0:1]
    for k in range(ROWS // 128):
        v = xz[k * 128:(k + 1) * 128].astype(F32)
        n = jnp.sum(v * v, axis=1, keepdims=True)
        at = k * SIDE + sub128 // SHARD
        at = at + core * (lax.rem(at, SIDE) * SIDE + at // SIDE - at)
        lane = lax.broadcasted_iota(I32, (128, 128), 1)
        size = jnp.sum(jnp.where(lane == z * COUNT + at // 2, bs, 0.0), axis=1, keepdims=True)
        inside = lax.rem(at, 2) * PAIR + core * SHARD + lax.rem(sub128, SHARD)
        ni[k * 128:(k + 1) * 128] = n + jnp.where(inside.astype(F32) >= size, FAR, 0.0)

    lane1 = lax.broadcasted_iota(I32, (1, 128), 1)
    row32 = lax.broadcasted_iota(I32, (SHARD, 128), 0)
    inside32 = [(lax.rem(chip, 2) * PAIR + c * SHARD + row32).astype(F32) for c in (core, 1 - core)]

    def owner(d):
        return lax.rem(z - d + 2 * OWNERS, OWNERS)

    def far_norms(g):
        parts = []
        for u0 in range(g * 8, g * 8 + 8, 4):
            units = []
            for u in range(u0, u0 + 4):
                s, side = UNITS[u]
                v = cols[u * SHARD:(u + 1) * SHARD].astype(F32)
                n = jnp.sum(v * v, axis=1, keepdims=True)
                block = owner(SLOTS[s]) * COUNT + half
                size = jnp.sum(jnp.where(lane1 == block, bs, 0.0), axis=1, keepdims=True)
                units.append(n + jnp.where(inside32[side] >= size, FAR, 0.0))
            n = jnp.concatenate(units, axis=0)
            parts.append(jnp.sum(jnp.where(sub128 == lane128, n, 0.0), axis=0, keepdims=True))
        return jnp.concatenate(parts, axis=1)

    def near(g):
        if g == 0:
            both = cols.at[pl.ds(0, PAIR)]
            pltpu.make_async_copy(both, both, loc_sem.at[0]).wait()
        if g != 2:
            come = cols.at[pl.ds(0, (GROUP - 1, GROUP, 0, 2 * GROUP)[g] * SHARD)]
            pltpu.make_async_copy(come, come, d_recv.at[min(g, 2)]).wait()
        nj = far_norms(g)
        for r in range(0, ROWS, 256):
            dots = lax.dot_general(xz[r:r + 256], cols[g * COLS:(g + 1) * COLS], (((1,), (1,)), ((), ())),
                                   preferred_element_type=F32)
            n = ni[r:r + 256]
            dist = jnp.concatenate([n, n], axis=1) + nj - 2.0 * dots
            kern[r:r + 256, g * COLS:(g + 1) * COLS] = jnp.exp(-dist)

    counts_in(2, -2)
    rows_in(2, -2)
    rows_in(1, -1)
    counts_in(5, -5)
    rows_in(5, -5)
    rows_in(3, -3)
    rest_in()

    slot1 = lane1 // COUNT
    own1 = jnp.zeros((1, 128), I32)
    for s, d in enumerate(SLOTS):
        own1 = jnp.where(slot1 == s, owner(d), own1)
    own1 = own1 * COUNT + lax.rem(lane1, COUNT)
    perm = jnp.where(sub128 == own1, 1.0, 0.0).astype(BF16)
    pick = jnp.where(lane8 == z * COUNT + sub8, 1.0, 0.0).astype(BF16)
    there = cm[...].reshape(OWNERS * COUNT, 128).astype(BF16)
    pairs = jnp.dot(cm[0].astype(BF16), perm, preferred_element_type=F32) + lax.dot_general(
        pick, there, (((1,), (1,)), ((), ())), preferred_element_type=F32)
    tsum[2 * CHIPS - 1] = pairs
    for i, (dx, dy, dc) in enumerate(MATES):
        pltpu.make_async_remote_copy(
            src_ref=tsum.at[2 * CHIPS - 1], dst_ref=tsum.at[i], send_sem=m_sem.at[0], recv_sem=m_sem.at[1],
            device_id=(z, place(dx, dy) * 2 + lax.rem(core + dc, 2)), device_id_type=MESH).start()
    near(0)
    near(1)
    rows_in(8, -8)
    rows_in(7, -7)
    rows_in(4, -4)
    rows_in(6, -6)
    near(2)
    mates = tsum.at[pl.ds(0, len(MATES))]
    pltpu.make_async_copy(mates, mates, m_sem.at[1]).wait()
    total = tsum[2 * CHIPS - 1]
    for i in range(len(MATES)):
        total = total + tsum[i]
    times = [jnp.sum(jnp.where(lane8 == s * COUNT + half, total, 0.0), axis=1, keepdims=True) for s in range(OWNERS)]
    for u in range(0, 2 * OWNERS, 4):
        four = [times[UNITS[u + k][0]] for k in range(4)]
        low = jnp.where(lane8 < SHARD, four[0], four[1])
        high = jnp.where(lane8 < 3 * SHARD, four[2], four[3])
        sg[:, u * SHARD:(u + 4) * SHARD] = jnp.where(lane8 < PAIR, low, high)

    def sums(row, c0, c1):
        k = kern[pl.ds(row * 128, 128), c0:c1]
        s = []
        for h in range(SIDE):
            block = (row * SIDE + h + core * (h * SIDE + row - row * SIDE - h)) // 2
            s.append(jnp.broadcast_to(sg[pl.ds(block, 1), c0:c1], (SHARD, c1 - c0)))
        s = jnp.concatenate(s, axis=0)
        w = s * k.astype(BF16).astype(F32)
        hi = w.astype(BF16)
        lo = (w - hi.astype(F32)).astype(BF16)
        far = cols[c0:c1]
        t = jnp.dot(hi, far, preferred_element_type=F32) + jnp.dot(lo, far, preferred_element_type=F32)
        m = s * k
        return t, sum(m[:, 128 * h:128 * (h + 1)] for h in range((c1 - c0) // 128))

    acc[ORDER[0]], fold[...] = sums(lax.rem(own_v + ORDER[0], SIDE), 0, 3 * COLS)
    near(3)

    lane32 = lax.broadcasted_iota(I32, (SHARD, 128), 1)
    sub32 = lax.broadcasted_iota(I32, (SHARD, 128), 0)

    def spot(step):
        return pl.ds(lax.rem(own_u + step, SIDE) * SHARD, SHARD)

    def send_to(src, dst, sem, du, dv, kind):
        pltpu.make_async_remote_copy(src_ref=src, dst_ref=dst, send_sem=sent.at[kind], recv_sem=sem,
                                     device_id=peer(du, dv), device_id_type=MESH).start()

    i = 0
    for dv in ORDER:
        if dv == ORDER[0]:
            t, m = sums(lax.rem(own_v + dv, SIDE), 3 * COLS, 4 * COLS)
            t, m = t + acc[dv], m + fold[...]
        else:
            t, m = sums(lax.rem(own_v + dv, SIDE), 0, 4 * COLS)
        acc[dv] = t
        if dv:
            send_v[dv - 1] = t[:, CUT:].astype(BF16)
            send_to(send_v.at[dv - 1], recv_v.at[dv - 1], r_recv.at[4], 0, dv, 4)
        for du in HOPS:
            send_u[du - 1, dv] = acc[dv, spot(du), :CUT].astype(BF16)
            send_to(send_u.at[du - 1, dv], recv_u.at[du - 1, dv], r_recv.at[dv], du, 0, 3)
        m = jnp.sum(m, axis=1, keepdims=True)
        mass[dv] = jnp.sum(jnp.where(sub128 == lane128, m, 0.0), axis=0, keepdims=True)
        for du in ORDER:
            if (du, dv) != (0, 0):
                send_to(mass.at[dv], mass.at[SIDE + i], a_recv.at[0], du, dv, 5)
                i += 1

    def come(ref, sem):
        pltpu.make_async_copy(ref, ref, sem).wait()

    def first_u(dv):
        come(recv_u.at[:, dv], r_recv.at[dv])
        r = acc[dv, spot(0), :CUT]
        for k in range(SIDE - 1):
            r = r + recv_u[k, dv].astype(F32)
        return r

    def along_v(dv):
        last_v[dv - 1] = first_u(dv)
        send_to(last_v.at[dv - 1], last_v.at[SIDE - 2 + dv], r_recv.at[6], 0, dv, 7)

    along_v(2)
    along_v(1)
    come(recv_v, r_recv.at[4])
    r = acc[0, :, CUT:]
    for k in range(SIDE - 1):
        r = r + recv_v[k].astype(F32)
    sum_v[...] = r
    for du in HOPS:
        last_u[du - 1] = sum_v[spot(du)]
        send_to(last_u.at[du - 1], last_u.at[SIDE - 2 + du], r_recv.at[5], du, 0, 6)
    along_v(3)
    r = first_u(0)
    a = mass[0]
    got = mass.at[pl.ds(SIDE, len(PEERS))]
    come(got, a_recv.at[0])
    for k in range(len(PEERS)):
        a = a + mass[SIDE + k]
    m = jnp.sum(jnp.where(lane32 == own_u * SHARD + sub32, a, 0.0), axis=1, keepdims=True)
    m = jnp.log(1.0 + m)
    log_ref[...] = jnp.sum(jnp.where(sub32 == lane32, m, 0.0), axis=0, keepdims=True)
    w = sum_v[spot(0)]
    there_u = last_u.at[pl.ds(SIDE - 1, SIDE - 1)]
    there_v = last_v.at[pl.ds(SIDE - 1, SIDE - 1)]
    come(there_u, r_recv.at[5])
    for k in range(SIDE - 1):
        w = w + last_u[SIDE - 1 + k]
    out_ref[:, CUT:] = w
    come(there_v, r_recv.at[6])
    for k in range(SIDE - 1):
        r = r + last_v[SIDE - 1 + k]
    out_ref[:, :CUT] = r
    shards = cols.at[pl.ds(0, (OWNERS - 1) * SHARD)]
    counted = cm.at[pl.ds(0, OWNERS - 1)]
    for what, sem in ((shards, sent.at[0]), (shards, sent.at[1]), (counted, sent.at[2]), (recv_u, sent.at[3]),
                      (recv_v, sent.at[4]), (got, sent.at[5]), (there_u, sent.at[6]), (there_v, sent.at[7]),
                      (mates, m_sem.at[0])):
        come(what, sem)


def body(embeddings, block_sizes, fetch_blocks, partners):
    hbm = pl.BlockSpec(memory_space=pltpu.HBM)
    vmem = pl.BlockSpec(memory_space=pltpu.VMEM)
    dma = pltpu.SemaphoreType.DMA
    edges = len(EDGES)
    room = ((0, 0), (0, 128 - OWNERS))
    ints = jnp.concatenate([
        block_sizes.reshape(1, 128),
        jnp.pad(fetch_blocks.reshape(1, OWNERS), room),
        jnp.pad(jnp.swapaxes(partners, 2, 3).reshape(4, OWNERS), room),
    ]).astype(F32)
    out, logs = pl.pallas_call(
        kernel,
        out_shape=(jax.ShapeDtypeStruct((SHARD, WIDTH), F32), jax.ShapeDtypeStruct((1, 128), F32)),
        in_specs=[hbm, vmem],
        out_specs=(vmem, vmem),
        scratch_shapes=[
            pltpu.VMEM((ROWS, WIDTH), BF16),
            pltpu.VMEM((OWNERS * PAIR, WIDTH), BF16),
            pltpu.VMEM((ROWS, OWNERS * PAIR), F32),
            pltpu.VMEM((SIDE, 128, WIDTH), F32),
            pltpu.VMEM((128, 128), F32),
            pltpu.VMEM((SIDE + len(PEERS), 1, 128), F32),
            pltpu.VMEM((ROWS, 128), F32),
            pltpu.VMEM((OWNERS, COUNT, 128), F32),
            pltpu.VMEM((2 * CHIPS, COUNT, 128), F32),
            pltpu.VMEM((COUNT, OWNERS * PAIR), F32),
            pltpu.VMEM((SIDE - 1, SIDE, SHARD, CUT), BF16),
            pltpu.VMEM((SIDE - 1, SIDE, SHARD, CUT), BF16),
            pltpu.VMEM((SIDE - 1, 128, WIDTH - CUT), BF16),
            pltpu.VMEM((SIDE - 1, 128, WIDTH - CUT), BF16),
            pltpu.VMEM((128, WIDTH - CUT), F32),
            pltpu.VMEM((2 * (SIDE - 1), SHARD, WIDTH - CUT), F32),
            pltpu.VMEM((2 * (SIDE - 1), SHARD, CUT), F32),
            dma((2,)),
            dma((8,)),
            dma((edges,)),
            dma((3,)),
            dma((len(COUNT_SEM) + 1,)),
            dma((2,)),
            dma((7,)),
            dma((1,)),
        ],
        compiler_params=pltpu.CompilerParams(collective_id=0, has_side_effects=True, vmem_limit_bytes=53 << 20),
        cost_estimate=pl.CostEstimate(flops=3 * 2 * 512 * 1024 * 768, bytes_accessed=4 << 20, transcendentals=512 * 1024),
    )(embeddings.reshape(CHIPS, 2, SHARD, WIDTH), ints)
    return out, logs[0, :SHARD]


def solution(mesh):
    return jax.shard_map(
        body,
        mesh=mesh,
        in_specs=(P("dp", None), P(), P("dp", "pair", None), P("dp", "pair", None, None)),
        out_specs=(P(("dp", "pair"), None), P(("dp", "pair"))),
        check_vma=False,
    )
```
